256 devices in a mesh: ang: 64 (over x, z_hi, y, core), slab: 4 (over z_lo).
Axes of the slice: x: 4, y: 4, z: 8 (z_hi: 2, z_lo: 4; z = z_hi * 4 + z_lo), core: 2. Of those that a mesh axis runs over, the one named last changes fastest.
Arguments:
- volume: float32 [2, 512, 16384], P(None, ('ang', 'slab')), may hold values from -6 to 6
- tv_split: float32 [3, 2, 512, 16384], P(None, None, ('ang', 'slab')), may hold values from -6 to 6
- tv_dual: float32 [3, 2, 512, 16384], P(None, None, ('ang', 'slab')), may hold values from -4 to 4
- measured: float32 [128, 8, 2, 64, 8, 128], P('ang', None, None, None, 'slab'), may hold values from -6 to 6
- fit_dual: float32 [128, 8, 2, 64, 8, 128], P('ang', None, None, None, 'slab'), may hold values from -4 to 4
- footprints: bfloat16 [40, 128, 128], replicated, may hold values from -0.1875 to 0.1875
- voxel_tile: int32 [128, 8, 8], replicated, may hold values from 0 to 127
- kernel_pick: int32 [128, 8, 8], replicated, may hold values from 0 to 39
- tile_count: int32 [128, 8], replicated, may hold values from 4 to 8
Outputs:
- volume_next: float32 [2, 512, 16384], P(None, ('ang', 'slab'))
- split_next: float32 [3, 2, 512, 16384], P(None, None, ('ang', 'slab'))
- tv_dual_next: float32 [3, 2, 512, 16384], P(None, None, ('ang', 'slab'))
- fit_dual_next: float32 [128, 8, 2, 64, 8, 128], P('ang', None, None, None, 'slab')
The draws below stay inside these ranges and needn't reach their ends.
Inputs may be any that keep to these rules, and one draw needn't show every extreme that they name: Only the first tile_count entries of a ray tile's list are live; tiles and kernels may repeat.
All inputs are finite; a program needn't handle non-finite values.
Results may differ from the reference program's by a relative error of at most 0.0068.
Values may be sent and summed in bfloat16 or wider, within the bound.
A program may use at most 128 MiB of HBM per device.

```python
import jax
import jax.numpy as jnp
from jax import lax

TILE_WIDTH = 128
VOLUME_CHANNELS = 2
KT = 128
RAY_TILE_COUNT = 8
NNZ = 8
NB = 40
DEVICE_SLICES = 2
NV = 16384
ANGLE_COUNT = 128
ZH = 64
ZL = 8
NZ = 512


def plant(entries, stream_key, smallest, largest):
    extent = entries.shape
    index_at = [jax.random.randint(jax.random.fold_in(stream_key, axis), (), 0, extent[axis]) for axis in range(len(extent))]
    entries = entries.at[tuple(index_at)].set(smallest)
    longest = extent.index(max(extent))
    index_at[longest] = (index_at[longest] + 1) % extent[longest]
    return entries.at[tuple(index_at)].set(largest)


def steps_of(stream_key, shape, shards, least, top_value):
    gain, own = 1.0, jax.random.fold_in(stream_key, 6)
    for dim, blocks in shards:
        heights = jnp.exp(jax.random.uniform(jax.random.fold_in(own, dim), (blocks,), jnp.float32, least / len(shards), top_value / len(shards)))
        gain = gain * jnp.repeat(heights, shape[dim] // blocks).reshape([-1 if axis == dim else 1 for axis in range(len(shape))])
    return gain


def bell_draw(key, extent, spread, most, shards=(), kind=jnp.bfloat16):
    entries = jax.random.normal(key, extent, jnp.float32) * spread
    if len(shards) > 0:
        entries = steps_of(key, extent, shards, -0.22, 0.18) * entries
    return jnp.clip(entries, min=-most, max=most).astype(kind)


def setup_inputs(seed: int = 0) -> dict:
    key_of = jax.random.split(jax.random.key(seed), 10)
    volume = bell_draw(key_of[0], (VOLUME_CHANNELS, NZ, NV), 1.0, 6.0, ((1, 256),), jnp.float32)
    tv_split = bell_draw(key_of[1], (3, VOLUME_CHANNELS, NZ, NV), 1.0, 6.0, ((2, 256),), jnp.float32)
    tv_dual = bell_draw(key_of[2], (3, VOLUME_CHANNELS, NZ, NV), 0.5, 4.0, ((2, 256),), jnp.float32)
    measured = bell_draw(key_of[3], (ANGLE_COUNT, RAY_TILE_COUNT, VOLUME_CHANNELS, ZH, ZL, TILE_WIDTH), 1.0, 6.0, ((0, 64), (4, 4)), jnp.float32)
    fit_dual = bell_draw(key_of[4], (ANGLE_COUNT, RAY_TILE_COUNT, VOLUME_CHANNELS, ZH, ZL, TILE_WIDTH), 0.5, 4.0, ((0, 64), (4, 4)), jnp.float32)
    footprints = bell_draw(key_of[5], (NB, TILE_WIDTH, TILE_WIDTH), (TILE_WIDTH * NNZ) ** -0.5, 0.1875)
    voxel_tile = plant(jax.random.randint(key_of[6], (ANGLE_COUNT, RAY_TILE_COUNT, NNZ), 0, KT), jax.random.fold_in(key_of[6], 1), 0, KT - 1).astype(jnp.int32)
    kernel_pick = plant(jax.random.randint(key_of[7], (ANGLE_COUNT, RAY_TILE_COUNT, NNZ), 0, NB), jax.random.fold_in(key_of[7], 1), 0, NB - 1).astype(jnp.int32)
    tile_count = plant(jax.random.randint(key_of[8], (ANGLE_COUNT, RAY_TILE_COUNT), NNZ // 2, NNZ + 1), jax.random.fold_in(key_of[8], 1), NNZ // 2, NNZ).astype(jnp.int32)
    return {"volume": volume, "tv_split": tv_split, "tv_dual": tv_dual, "measured": measured, "fit_dual": fit_dual, "footprints": footprints, "voxel_tile": voxel_tile, "kernel_pick": kernel_pick, "tile_count": tile_count}


data_fit_penalty = 1.0
penalty_tv = 0.5
tv_weight = 0.3
step_size = 0.3


def differences(image, above_slice, slice_keep):
    grid = image.reshape(VOLUME_CHANNELS, -1, KT, TILE_WIDTH)
    upper = jnp.concatenate([grid[:, 1:], above_slice.reshape(VOLUME_CHANNELS, 1, KT, TILE_WIDTH)], axis=1)
    along_slices = (upper - grid) * slice_keep[None, :, None, None]
    along_rows = jnp.concatenate([grid[:, :, 1:] - grid[:, :, :-1], jnp.zeros_like(grid[:, :, :1])], axis=2)
    along_cols = jnp.concatenate([grid[..., 1:] - grid[..., :-1], jnp.zeros_like(grid[..., :1])], axis=3)
    return jnp.stack([along_slices, along_rows, along_cols]).reshape(3, VOLUME_CHANNELS, -1, KT * TILE_WIDTH)


def adjoint(terms, slice_keep):
    parts = terms.reshape(3, VOLUME_CHANNELS, -1, KT, TILE_WIDTH)
    slice_part = parts[0] * slice_keep[None, :, None, None]
    below_slice = jnp.zeros_like(slice_part[:, :1])
    result = jnp.concatenate([below_slice, slice_part[:, :-1]], axis=1) - slice_part
    row_part = parts[1]
    result = result + jnp.concatenate([jnp.zeros_like(row_part[:, :, :1]), row_part[:, :, :-1]], axis=2)
    result = result - jnp.concatenate([row_part[:, :, :-1], jnp.zeros_like(row_part[:, :, :1])], axis=2)
    col_part = parts[2]
    result = result + jnp.concatenate([jnp.zeros_like(col_part[..., :1]), col_part[..., :-1]], axis=3)
    result = result - jnp.concatenate([col_part[..., :-1], jnp.zeros_like(col_part[..., :1])], axis=3)
    return result.reshape(VOLUME_CHANNELS, -1, KT * TILE_WIDTH)


def reference(volume, tv_split, tv_dual, measured, fit_dual, footprints, voxel_tile, kernel_pick, tile_count):
    tile_code = (voxel_tile * NB + kernel_pick).reshape(ANGLE_COUNT * RAY_TILE_COUNT, NNZ).astype(jnp.int32)
    entry_index = jnp.arange(NNZ, dtype=jnp.int32)
    live = (entry_index[None, :] < tile_count.reshape(ANGLE_COUNT * RAY_TILE_COUNT, 1)).astype(jnp.float32)
    device_groups = NZ // DEVICE_SLICES
    volume_by_group = jnp.moveaxis(volume.reshape(VOLUME_CHANNELS, device_groups, DEVICE_SLICES, NV), 1, 0)
    measurement_by_group = jnp.moveaxis(measured.reshape(ANGLE_COUNT, RAY_TILE_COUNT, VOLUME_CHANNELS, device_groups, DEVICE_SLICES, TILE_WIDTH), 3, 0)
    dual_by_group = jnp.moveaxis(fit_dual.reshape(ANGLE_COUNT, RAY_TILE_COUNT, VOLUME_CHANNELS, device_groups, DEVICE_SLICES, TILE_WIDTH), 3, 0)
    bank_float = footprints.astype(jnp.float32)

    def single_group(group_pieces):
        volume_shard, measurement_shard, dual_shard = group_pieces
        vol_low = volume_shard.astype(jnp.bfloat16).reshape(VOLUME_CHANNELS, DEVICE_SLICES, KT, TILE_WIDTH)
        tile_bank = jnp.einsum("czkt,btu->kbczu", vol_low.astype(jnp.float32), bank_float)
        tile_bank = tile_bank.astype(jnp.bfloat16).reshape(KT * NB, VOLUME_CHANNELS * DEVICE_SLICES * TILE_WIDTH).astype(jnp.float32)
        proj = jnp.zeros((ANGLE_COUNT * RAY_TILE_COUNT, VOLUME_CHANNELS * DEVICE_SLICES * TILE_WIDTH), jnp.float32)
        for entry in range(NNZ):
            proj = proj + tile_bank[tile_code[:, entry]] * live[:, entry:entry + 1]
        proj = proj.astype(jnp.bfloat16)
        projector_float = proj.reshape(ANGLE_COUNT, RAY_TILE_COUNT, VOLUME_CHANNELS, DEVICE_SLICES, TILE_WIDTH).astype(jnp.float32)
        data_fit_value = (measurement_shard + data_fit_penalty * projector_float + dual_shard) / (1.0 + data_fit_penalty)
        dual_next = dual_shard + data_fit_penalty * (projector_float - data_fit_value)
        residual = (projector_float - data_fit_value + dual_next / data_fit_penalty).astype(jnp.bfloat16)
        res_rows = residual.reshape(ANGLE_COUNT * RAY_TILE_COUNT, VOLUME_CHANNELS * DEVICE_SLICES * TILE_WIDTH).astype(jnp.float32)
        grouped = jnp.zeros((KT * NB, VOLUME_CHANNELS * DEVICE_SLICES * TILE_WIDTH), jnp.float32)
        for entry in range(NNZ):
            grouped = grouped + jax.ops.segment_sum(res_rows * live[:, entry:entry + 1], tile_code[:, entry], num_segments=KT * NB)
        grouped = grouped.astype(jnp.bfloat16).reshape(KT, NB, VOLUME_CHANNELS, DEVICE_SLICES, TILE_WIDTH)
        back_part = jnp.einsum("kbczu,btu->czkt", grouped.astype(jnp.float32), bank_float)
        return back_part.reshape(VOLUME_CHANNELS, DEVICE_SLICES, NV), dual_next

    backprojected_full, dual_gathered = lax.map(single_group, (volume_by_group, measurement_by_group, dual_by_group))
    back_proj = jnp.moveaxis(backprojected_full, 0, 1).reshape(VOLUME_CHANNELS, NZ, NV)
    fit_dual_next = jnp.moveaxis(dual_gathered, 0, 3).reshape(ANGLE_COUNT, RAY_TILE_COUNT, VOLUME_CHANNELS, ZH, ZL, TILE_WIDTH)

    slice_keep = (jnp.arange(NZ, dtype=jnp.int32) < NZ - 1).astype(jnp.float32)
    no_slice = jnp.zeros((VOLUME_CHANNELS, 1, NV), jnp.float32)
    terms = differences(volume, no_slice, slice_keep) - tv_split + tv_dual / penalty_tv
    descent = back_proj + penalty_tv * adjoint(terms, slice_keep)
    volume_next = volume - step_size * descent
    diff_next = differences(volume_next, no_slice, slice_keep)
    shrink_arg = diff_next + tv_dual / penalty_tv
    split_next = jnp.sign(shrink_arg) * jnp.maximum(jnp.abs(shrink_arg) - tv_weight / penalty_tv, 0.0)
    tv_dual_next = tv_dual + penalty_tv * (diff_next - split_next)
    return volume_next, split_next, tv_dual_next, fit_dual_next
```

```python
import jax
import jax.numpy as jnp
from jax import lax
from jax.experimental import pallas as pl
from jax.experimental.pallas import tpu as pltpu
from jax.sharding import PartitionSpec as P

TILE_WIDTH = 128
VOLUME_CHANNELS = 2
KT = 128
NB = 40
NNZ = 8
RAYS = 8
PEERS = 32
ROWS = 16
PLANES = 4
ALL_ROWS = PEERS * ROWS
DEAD = NB * KT

penalty_tv = 0.5
tv_weight = 0.3
step_size = 0.3

F32 = jnp.float32
BF16 = jnp.bfloat16
MESH = pl.DeviceIdType.MESH


def kernel(
    codes, code_lanes, vol_hbm, split_hbm, tvd_hbm, meas_hbm, dual_hbm, foot_hbm,
    vol_out, split_out, tvd_out, fit_out,
    vol_v, split_v, tvd_v, meas_v, dual_v, foot_v,
    foot_wide, vol_send, vol_recv, vol_rows, vol_low, bank, counts, grouped,
    meas_send, meas_recv, proj_send, proj_recv, resid, ray_rows,
    first_send, first_recv, last_send, last_recv, part_send, part_recv, back_own, adj_v,
    next_send, next_recv,
    local_sem, out_sem, meas_ssem, meas_rsem, proj_ssem, proj_rsem, one_ssem, one_rsem,
):
    ang = lax.axis_index("ang")
    slab = lax.axis_index("slab")
    xi = ang // 16
    half = (ang // 8) % 2
    wi = ang % 8
    yi = wi // 2
    core = wi % 2
    me = xi * 8 + wi
    other = (xi * 16 + (1 - half) * 8 + wi, slab)
    pos = ang * 4 + slab
    up = (pos + 1) % 256
    down = (pos + 255) % 256
    up_id = (up // 4, up % 4)
    down_id = (down // 4, down % 4)
    keep = (pos < 255).astype(F32)
    keep_below = (pos > 0).astype(F32)

    def peer_of(i):
        px = (xi + i // 8) % 4
        py = (yi + (i // 2) % 4) % 4
        pc = (core + i % 2) % 2
        return px, py * 2 + pc

    local = [
        pltpu.make_async_copy(vol_hbm, vol_v, local_sem.at[0]),
        pltpu.make_async_copy(meas_hbm, meas_v, local_sem.at[1]),
        pltpu.make_async_copy(split_hbm, split_v, local_sem.at[2]),
        pltpu.make_async_copy(tvd_hbm, tvd_v, local_sem.at[3]),
        pltpu.make_async_copy(foot_hbm, foot_v, local_sem.at[4]),
        pltpu.make_async_copy(dual_hbm, dual_v, local_sem.at[5]),
    ]
    for copy in local:
        copy.start()

    barrier = pltpu.get_barrier_semaphore()

    @pl.loop(1, PEERS)
    def _(i):
        px, pw = peer_of(i)
        pl.semaphore_signal(
            barrier, inc=1, device_id=(px * 16 + half * 8 + pw, slab), device_id_type=MESH
        )

    for device in (other, up_id, down_id):
        pl.semaphore_signal(barrier, inc=1, device_id=device, device_id_type=MESH)

    def plane(ref, lead, z):
        return ref[pl.ds(lead * 256 + z, KT, stride=2), :]

    local[0].wait()
    for z in range(2):
        for c in range(2):
            cz = z * 2 + c
            image = plane(vol_v, c, z)
            vol_rows[pl.ds(cz, KT, stride=8), :] = image
            vol_send[cz] = image.astype(BF16)

    pl.semaphore_wait(barrier, PEERS + 2)

    def remote(src, dst, slot, device):
        return pltpu.make_async_remote_copy(
            src_ref=src, dst_ref=dst, send_sem=one_ssem.at[slot], recv_sem=one_rsem.at[slot],
            device_id=device, device_id_type=MESH,
        )

    vol_copy = remote(vol_send, vol_recv, 0, other)
    vol_copy.start()
    first_copy = remote(vol_send.at[pl.ds(0, 2)], first_recv, 1, down_id)
    first_copy.start()

    local[1].wait()

    def slice_row(px, pw, part, z, c):
        zh = px * 16 + ((half + part) % 2) * 8 + pw
        return c * 128 + zh * 2 + z

    def message(px, pw):
        peer = px * 8 + pw
        for part in range(2):
            for z in range(2):
                for c in range(2):
                    start = slice_row(px, pw, part, z, c)
                    rows = meas_v[pl.ds(start, ROWS, stride=256), :]
                    meas_send[peer, part * 4 + z * 2 + c] = rows.astype(BF16)

    def exchange(send, recv, ssem, rsem, px, pw):
        return pltpu.make_async_remote_copy(
            src_ref=send.at[px * 8 + pw], dst_ref=recv.at[me],
            send_sem=ssem.at[px * 8 + pw], recv_sem=rsem.at[me],
            device_id=(px * 16 + half * 8 + pw, slab), device_id_type=MESH,
        )

    def arrival(send, recv, ssem, rsem, px, pw):
        return pltpu.make_async_remote_copy(
            src_ref=send.at[px * 8 + pw], dst_ref=recv.at[px * 8 + pw],
            send_sem=ssem.at[px * 8 + pw], recv_sem=rsem.at[px * 8 + pw],
            device_id=(px * 16 + half * 8 + pw, slab), device_id_type=MESH,
        )

    @pl.loop(1, PEERS)
    def _(i):
        px, pw = peer_of(i)
        message(px, pw)
        exchange(meas_send, meas_recv, meas_ssem, meas_rsem, px, pw).start()

    message(xi, wi)
    for cz in range(8):
        meas_recv[me, cz] = meas_send[me, cz]

    local[2].wait()
    local[3].wait()
    for c in range(2):
        term = plane(tvd_v, c, 1) / penalty_tv - plane(split_v, c, 1) - plane(vol_v, c, 1)
        last_send[c] = term.astype(BF16)
    last_copy = remote(last_send, last_recv, 2, up_id)
    last_copy.start()

    @pl.loop(0, 32)
    def _(step):
        kc = step // 4
        lt = step % 4
        lanes = pl.ds(pl.multiple_of(lt * 128, 128), 128)
        tile = lax.broadcasted_iota(jnp.int32, (16, 128), 0) + kc * 16
        picks = []
        for j in range(NNZ):
            code = jnp.broadcast_to(code_lanes[j:j + 1, lanes], (16, 128))
            pick = jnp.where((code % 128) == tile, code // 128, -1)
            picks.append(pick.astype(F32).astype(BF16))
        one = jnp.ones((16, 128), BF16)
        zero = jnp.zeros((16, 128), BF16)
        for b in range(NB):
            hits = [jnp.where(pick == jnp.asarray(b, BF16), one, zero) for pick in picks]
            while len(hits) > 1:
                hits = [hits[n] + hits[n + 1] for n in range(0, len(hits), 2)]
            counts[pl.ds(pl.multiple_of(b * 128 + kc * 16, 16), 16), lanes] = hits[0]

    local[4].wait()
    for b in range(NB):
        foot_wide[:, b * 128:(b + 1) * 128] = foot_v[b]

    vol_copy.wait_recv()
    for cz in range(PLANES):
        vol_rows[pl.ds(4 + cz, KT, stride=8), :] = vol_recv[cz].astype(F32)
    vol_low[...] = vol_rows[...].astype(BF16)

    @pl.loop(0, NB // 2)
    def _(step):
        cols = pl.ds(pl.multiple_of(step * 256, 256), 256)
        for part in range(4):
            out = jnp.dot(
                vol_low[part * 256:(part + 1) * 256, :], foot_wide[:, cols],
                preferred_element_type=F32,
            )
            for n in range(2):
                bank[pl.ds((step * 2 + n) * 128 + part * 32, 32)] = (
                    out[:, n * 128:(n + 1) * 128].reshape(32, 8, 128)
                )

    bank[DEAD] = jnp.zeros((8, 128), F32)

    def project(px, pw):
        peer = px * 8 + pw
        for row in range(ROWS):
            at = peer * (ROWS * NNZ) + row * NNZ
            got = [bank[codes[at + j]] for j in range(NNZ)]
            while len(got) > 1:
                got = [got[n] + got[n + 1] for n in range(0, len(got), 2)]
            ray_rows[row * 8:(row + 1) * 8, :] = got[0]
        for cz in range(8):
            proj_send[peer, cz] = ray_rows[pl.ds(cz, ROWS, stride=8), :].astype(BF16)

    @pl.loop(1, PEERS)
    def _(i):
        px, pw = peer_of(i)
        project(px, pw)
        exchange(proj_send, proj_recv, proj_ssem, proj_rsem, px, pw).start()

    project(xi, wi)
    for cz in range(8):
        proj_recv[me, cz] = proj_send[me, cz]

    def subtract(px, pw):
        peer = px * 8 + pw
        rows = pl.ds(pl.multiple_of(peer * ROWS, ROWS), ROWS)
        for cz in range(8):
            gap = proj_send[peer, cz].astype(F32) - meas_recv[peer, cz].astype(F32)
            resid[cz // 4, rows, (cz % 4) * 128:(cz % 4 + 1) * 128] = gap.astype(BF16)

    subtract(xi, wi)

    @pl.loop(1, PEERS)
    def _(i):
        px, pw = peer_of(i)
        arrival(meas_send, meas_recv, meas_ssem, meas_rsem, px, pw).wait_recv()
        subtract(px, pw)

    def backward(part):
        @pl.loop(0, NB // 2)
        def _(step):
            rows = pl.ds(pl.multiple_of(step * 256, 256), 256)
            out = jnp.dot(counts[rows, :], resid[part], preferred_element_type=F32).astype(BF16)
            for n in range(2):
                cols = pl.ds(pl.multiple_of((step * 2 + n) * 128, 128), 128)
                for cz in range(PLANES):
                    grouped[cz * 128:(cz + 1) * 128, cols] = (
                        out[n * 128:(n + 1) * 128, cz * 128:(cz + 1) * 128]
                    )
        return lax.dot_general(
            grouped[...], foot_wide[...], (((1,), (1,)), ((), ())), preferred_element_type=F32
        )

    theirs = backward(1)
    for cz in range(PLANES):
        part_send[cz] = theirs[cz * 128:(cz + 1) * 128, :].astype(BF16)
    part_copy = remote(part_send, part_recv, 3, other)
    part_copy.start()
    back_own[...] = backward(0)

    row_at = lax.broadcasted_iota(jnp.int32, (KT, TILE_WIDTH), 0)
    col_at = lax.broadcasted_iota(jnp.int32, (KT, TILE_WIDTH), 1)
    inner_row = row_at < KT - 1
    inner_col = col_at < TILE_WIDTH - 1

    def along(image, axis):
        step = pltpu.roll(image, 127, axis) - image
        return jnp.where(inner_row if axis == 0 else inner_col, step, 0.0)

    def spread(part, axis):
        part = jnp.where(inner_row if axis == 0 else inner_col, part, 0.0)
        return pltpu.roll(part, 1, axis) - part

    def force(i, c, z):
        return plane(tvd_v, i * 2 + c, z) / penalty_tv - plane(split_v, i * 2 + c, z)

    first_copy.wait_recv()
    last_copy.wait_recv()
    for c in range(2):
        images = [plane(vol_v, c, z) for z in range(2)]
        below = (last_recv[c].astype(F32) + images[0]) * keep_below
        middle = images[1] - images[0] + force(0, c, 0)
        above = (first_recv[c].astype(F32) - images[1] + force(0, c, 1)) * keep
        for z, slices in enumerate((below - middle, middle - above)):
            total = slices
            for axis in range(2):
                total = total + spread(along(images[z], axis) + force(1 + axis, c, z), axis)
            adj_v[z * 2 + c] = penalty_tv * total

    part_copy.wait_recv()
    for z in range(2):
        for c in range(2):
            cz = z * 2 + c
            descent = back_own[cz * 128:(cz + 1) * 128, :] + part_recv[cz].astype(F32) + adj_v[cz]
            image = plane(vol_v, c, z) - step_size * descent
            vol_v[pl.ds(c * 256 + z, KT, stride=2), :] = image
            if z == 0:
                next_send[c] = image.astype(BF16)
        if z == 0:
            next_copy = remote(next_send, next_recv, 4, down_id)
            next_copy.start()
    vol_done = pltpu.make_async_copy(vol_v, vol_out, out_sem.at[0])
    vol_done.start()

    local[5].wait()

    def fit(px, pw):
        peer = px * 8 + pw
        for part in range(2):
            for z in range(2):
                for c in range(2):
                    rows = pl.ds(slice_row(px, pw, part, z, c), ROWS, stride=256)
                    proj = proj_recv[peer, part * 4 + z * 2 + c].astype(F32)
                    dual_v[rows, :] = 0.5 * (proj + dual_v[rows, :] - meas_v[rows, :])

    fit(xi, wi)

    @pl.loop(1, PEERS)
    def _(i):
        px, pw = peer_of(i)
        arrival(proj_send, proj_recv, proj_ssem, proj_rsem, px, pw).wait_recv()
        fit(px, pw)

    fit_done = pltpu.make_async_copy(dual_v, fit_out, out_sem.at[1])
    fit_done.start()

    next_copy.wait_recv()
    for c in range(2):
        images = [plane(vol_v, c, z) for z in range(2)]
        above = (next_recv[c].astype(F32) - images[1]) * keep
        for z, slices in enumerate((images[1] - images[0], above)):
            steps = (slices, along(images[z], 0), along(images[z], 1))
            for i in range(3):
                rows = pl.ds((i * 2 + c) * 256 + z, KT, stride=2)
                dual = tvd_v[rows, :]
                arg = steps[i] + dual / penalty_tv
                bound = tv_weight / penalty_tv
                split = arg - jnp.clip(arg, -bound, bound)
                split_v[rows, :] = split
                tvd_v[rows, :] = dual + penalty_tv * (steps[i] - split)
    split_done = pltpu.make_async_copy(split_v, split_out, out_sem.at[2])
    split_done.start()
    tvd_done = pltpu.make_async_copy(tvd_v, tvd_out, out_sem.at[3])
    tvd_done.start()

    for copy in (vol_copy, first_copy, last_copy, part_copy, next_copy):
        copy.wait_send()

    @pl.loop(1, PEERS)
    def _(i):
        px, pw = peer_of(i)
        exchange(meas_send, meas_recv, meas_ssem, meas_rsem, px, pw).wait_send()
        exchange(proj_send, proj_recv, proj_ssem, proj_rsem, px, pw).wait_send()

    for copy in (vol_done, fit_done, split_done, tvd_done):
        copy.wait()


def to_rows(array):
    lead = array.shape[:-2]
    tiles = array.reshape(*lead, 2, KT, TILE_WIDTH)
    return jnp.swapaxes(tiles, -3, -2).reshape(-1, TILE_WIDTH)


def from_rows(rows, shape):
    tiles = rows.reshape(*shape[:-2], KT, 2, TILE_WIDTH)
    return jnp.swapaxes(tiles, -3, -2).reshape(shape)


def shards(
    volume, tv_split, tv_dual, measured, fit_dual, footprints, voxel_tile, kernel_pick, tile_count
):
    half = (lax.axis_index("ang") // 8) % 2
    code = kernel_pick * KT + voxel_tile
    live = jnp.arange(NNZ, dtype=jnp.int32) < tile_count[:, :, None]
    code = jnp.where(live, code, DEAD).reshape(4, 2, 16, RAYS, NNZ)
    code = lax.dynamic_index_in_dim(code, half, 1, keepdims=False).reshape(ALL_ROWS, NNZ)

    hbm = pl.BlockSpec(memory_space=pl.ANY)
    vmem = pl.BlockSpec(memory_space=pltpu.VMEM)
    tile = (KT, TILE_WIDTH)
    volume_next, split_next, tv_dual_next, fit_dual_next = pl.pallas_call(
        kernel,
        out_shape=[
            jax.ShapeDtypeStruct((512, 128), F32),
            jax.ShapeDtypeStruct((1536, 128), F32),
            jax.ShapeDtypeStruct((1536, 128), F32),
            jax.ShapeDtypeStruct((4096, 128), F32),
        ],
        in_specs=[pl.BlockSpec(memory_space=pltpu.SMEM), vmem] + [hbm] * 6,
        out_specs=[hbm] * 4,
        scratch_shapes=[
            pltpu.VMEM((512, 128), F32),
            pltpu.VMEM((1536, 128), F32),
            pltpu.VMEM((1536, 128), F32),
            pltpu.VMEM((4096, 128), F32),
            pltpu.VMEM((4096, 128), F32),
            pltpu.VMEM((NB, 128, 128), BF16),
            pltpu.VMEM((128, NB * 128), BF16),
            pltpu.VMEM((PLANES, *tile), BF16),
            pltpu.VMEM((PLANES, *tile), BF16),
            pltpu.VMEM((1024, 128), F32),
            pltpu.VMEM((1024, 128), BF16),
            pltpu.VMEM((NB * KT + 8, 8, 128), F32),
            pltpu.VMEM((NB * KT, ALL_ROWS), BF16),
            pltpu.VMEM((512, NB * 128), BF16),
            pltpu.VMEM((PEERS, 8, ROWS, 128), BF16),
            pltpu.VMEM((PEERS, 8, ROWS, 128), BF16),
            pltpu.VMEM((PEERS, 8, ROWS, 128), BF16),
            pltpu.VMEM((PEERS, 8, ROWS, 128), BF16),
            pltpu.VMEM((2, ALL_ROWS, 512), BF16),
            pltpu.VMEM((ROWS * 8, 128), F32),
            pltpu.VMEM((2, *tile), BF16),
            pltpu.VMEM((2, *tile), BF16),
            pltpu.VMEM((2, *tile), BF16),
            pltpu.VMEM((2, *tile), BF16),
            pltpu.VMEM((PLANES, *tile), BF16),
            pltpu.VMEM((PLANES, *tile), BF16),
            pltpu.VMEM((512, 128), F32),
            pltpu.VMEM((PLANES, *tile), F32),
            pltpu.VMEM((2, *tile), BF16),
            pltpu.VMEM((2, *tile), BF16),
            pltpu.SemaphoreType.DMA((6,)),
            pltpu.SemaphoreType.DMA((4,)),
            pltpu.SemaphoreType.DMA((PEERS,)),
            pltpu.SemaphoreType.DMA((PEERS,)),
            pltpu.SemaphoreType.DMA((PEERS,)),
            pltpu.SemaphoreType.DMA((PEERS,)),
            pltpu.SemaphoreType.DMA((5,)),
            pltpu.SemaphoreType.DMA((5,)),
        ],
        compiler_params=pltpu.CompilerParams(
            collective_id=0, has_side_effects=True, vmem_limit_bytes=60 * 1024 * 1024
        ),
    )(
        code.reshape(-1), code.T,
        to_rows(volume), to_rows(tv_split), to_rows(tv_dual),
        measured.reshape(4096, 128), fit_dual.reshape(4096, 128), footprints,
    )
    return (
        from_rows(volume_next, volume.shape),
        from_rows(split_next, tv_split.shape),
        from_rows(tv_dual_next, tv_dual.shape),
        fit_dual_next.reshape(fit_dual.shape),
    )


def solution(mesh):
    return jax.shard_map(
        shards,
        mesh=mesh,
        in_specs=(
            P(None, ("ang", "slab"), None),
            P(None, None, ("ang", "slab"), None),
            P(None, None, ("ang", "slab"), None),
            P("ang", None, None, None, "slab", None),
            P("ang", None, None, None, "slab", None),
            P(),
            P(),
            P(),
            P(),
        ),
        out_specs=(
            P(None, ("ang", "slab"), None),
            P(None, None, ("ang", "slab"), None),
            P(None, None, ("ang", "slab"), None),
            P("ang", None, None, None, "slab", None),
        ),
        check_vma=False,
    )
```

```python
import jax
import jax.numpy as jnp
from jax import lax
from jax.experimental import pallas as pl
from jax.experimental.pallas import tpu as pltpu
from jax.sharding import PartitionSpec as P

TILE_WIDTH = 128
VOLUME_CHANNELS = 2
KT = 128
NB = 40
NNZ = 8
RAYS = 8
PEERS = 32
ROWS = 16
PLANES = 4
ALL_ROWS = PEERS * ROWS
DEAD = NB * KT
RUNS = 4
RUN = KT // RUNS
TALL = 8

penalty_tv = 0.5
tv_weight = 0.3
step_size = 0.3

F32 = jnp.float32
BF16 = jnp.bfloat16
MESH = pl.DeviceIdType.MESH


def kernel(
    tile_ref, pick_ref, live_ref, vol_hbm, split_hbm, tvd_hbm, meas_hbm, dual_hbm, foot_hbm,
    vol_out, split_out, tvd_out, fit_out,
    vol_v, split_v, tvd_v, meas_v, dual_v, foot_v,
    foot_wide, vol_send, vol_recv, vol_rows, bank, counts, grouped,
    meas_send, meas_recv, proj_send, proj_recv, resid, ray_rows,
    first_recv, last_send, last_recv, part_send, part_recv, back_own, adj_v,
    next_send, next_recv, code_v, codes, lanes_v,
    local_sem, out_sem, meas_ssem, meas_rsem, proj_ssem, proj_rsem, one_ssem, one_rsem,
):
    ang = lax.axis_index("ang")
    slab = lax.axis_index("slab")
    xi = ang // 16
    half = (ang // 8) % 2
    wi = ang % 8
    yi = wi // 2
    core = wi % 2
    me = xi * 8 + wi
    other = (xi * 16 + (1 - half) * 8 + wi, slab)
    pos = ang * 4 + slab
    up = (pos + 1) % 256
    down = (pos + 255) % 256
    up_id = (up // 4, up % 4)
    down_id = (down // 4, down % 4)
    keep = (pos < 255).astype(F32)
    keep_below = (pos > 0).astype(F32)

    def peer_of(i):
        n = i % 16
        px = (xi + 4 - n % 4) % 4
        py = (yi + 8 - n % 4 - n // 4) % 4
        pc = (core + i // 16) % 2
        return px, py * 2 + pc

    def far_peer(i):
        px = (xi + 6 - i // 8) % 4
        py = (yi + 6 - i // 2 % 4) % 4
        return px, py * 2 + i % 2

    def ang_of(px, pw):
        return px * 16 + half * 8 + pw

    local = [
        pltpu.make_async_copy(vol_hbm, vol_v, local_sem.at[0]),
        pltpu.make_async_copy(meas_hbm, meas_v, local_sem.at[1]),
        pltpu.make_async_copy(split_hbm, split_v, local_sem.at[2]),
        pltpu.make_async_copy(tvd_hbm, tvd_v, local_sem.at[3]),
        pltpu.make_async_copy(foot_hbm, foot_v, local_sem.at[4]),
        pltpu.make_async_copy(dual_hbm, dual_v, local_sem.at[5]),
    ]
    for copy in local:
        copy.start()

    barrier = pltpu.get_barrier_semaphore()

    pl.semaphore_signal(barrier, inc=1, device_id=other, device_id_type=MESH)

    @pl.loop(0, PEERS)
    def _(i):
        px, pw = far_peer(i)

        @pl.when(px * 8 + pw != me)
        def _():
            pl.semaphore_signal(
                barrier, inc=1, device_id=(ang_of(px, pw), slab), device_id_type=MESH
            )

    for device in (up_id, down_id):
        pl.semaphore_signal(barrier, inc=1, device_id=device, device_id_type=MESH)

    def plane(ref, lead, z):
        return ref[pl.ds(lead * 256 + z, KT, stride=2), :]

    local[0].wait()
    for z in range(2):
        for c in range(2):
            cz = z * 2 + c
            image = plane(vol_v, c, z)
            vol_rows[pl.ds(c * 2 + z, KT, stride=8), :] = image
            for run in range(RUNS):
                vol_send[run, cz] = image[run * RUN:(run + 1) * RUN, :].astype(BF16)

    local[1].wait()

    def slice_row(px, pw, part, z, c):
        zh = px * 16 + ((half + part) % 2) * 8 + pw
        return c * 128 + zh * 2 + z

    def message(px, pw):
        peer = px * 8 + pw
        for part in range(2):
            for z in range(2):
                for c in range(2):
                    start = slice_row(px, pw, part, z, c)
                    rows = meas_v[pl.ds(start, ROWS, stride=256), :]
                    meas_send[peer, part * 4 + z * 2 + c] = rows.astype(BF16)

    @pl.loop(0, PEERS)
    def _(peer):
        message(peer // 8, peer % 8)

    for cz in range(8):
        meas_recv[me, cz] = meas_send[me, cz]

    def exchange(send, recv, ssem, rsem, px, pw):
        return pltpu.make_async_remote_copy(
            src_ref=send.at[px * 8 + pw], dst_ref=recv.at[me],
            send_sem=ssem.at[px * 8 + pw], recv_sem=rsem.at[me],
            device_id=(ang_of(px, pw), slab), device_id_type=MESH,
        )

    def arrival(send, recv, ssem, rsem, px, pw):
        return pltpu.make_async_remote_copy(
            src_ref=send.at[px * 8 + pw], dst_ref=recv.at[px * 8 + pw],
            send_sem=ssem.at[px * 8 + pw], recv_sem=rsem.at[px * 8 + pw],
            device_id=(ang_of(px, pw), slab), device_id_type=MESH,
        )

    pl.semaphore_wait(barrier, PEERS + 2)

    def remote(src, dst, slot, device):
        return pltpu.make_async_remote_copy(
            src_ref=src, dst_ref=dst, send_sem=one_ssem.at[slot], recv_sem=one_rsem.at[slot],
            device_id=device, device_id_type=MESH,
        )

    vol_copies = [
        remote(vol_send.at[run], vol_recv.at[run], run, other) for run in range(RUNS)
    ]
    for copy in vol_copies:
        copy.start()

    @pl.loop(1, PEERS)
    def _(i):
        px, pw = peer_of(i)
        exchange(meas_send, meas_recv, meas_ssem, meas_rsem, px, pw).start()

    entry_at = lax.broadcasted_iota(jnp.int32, (NNZ, 128), 0)
    lane = lax.broadcasted_iota(jnp.int32, (128, ALL_ROWS), 1)
    angle_at = lax.broadcasted_iota(jnp.int32, (128, ALL_ROWS), 0)
    peer_at = lane // ROWS
    wanted = peer_at // 8 * 32 + half * 16 + peer_at % 8 * 2 + lane // RAYS % 2
    same_angle = wanted == angle_at
    found = jnp.zeros((2 * NNZ, ALL_ROWS), F32)
    for r in range(RAYS):
        rows = slice(r * NNZ, (r + 1) * NNZ)
        is_live = entry_at < live_ref[r:r + 1, :]
        tiles = tile_ref[rows, :]
        picks = jnp.where(is_live, pick_ref[rows, :], NB)
        code_v[rows, :] = jnp.where(is_live, picks * KT + tiles, DEAD)
        both = jnp.concatenate([tiles, picks], axis=0).astype(F32).astype(BF16)
        chosen = jnp.where(same_angle & (lane % RAYS == r), 1.0, 0.0).astype(BF16)
        found = found + jnp.dot(both, chosen, preferred_element_type=F32)
    lanes_v[...] = found
    codes_copy = pltpu.make_async_copy(code_v, codes, local_sem.at[6])
    codes_copy.start()

    local[4].wait()
    for b in range(NB):
        foot_wide[:, b * 128:(b + 1) * 128] = foot_v[b]

    @pl.loop(0, 32)
    def _(step):
        kc = step // 4
        lt = step % 4
        lanes = pl.ds(pl.multiple_of(lt * 128, 128), 128)
        tile = (lax.broadcasted_iota(jnp.int32, (16, 128), 0) + kc * 16).astype(F32)
        picks = []
        for j in range(NNZ):
            held = jnp.broadcast_to(lanes_v[j:j + 1, lanes], (16, 128)) == tile
            pick = jnp.broadcast_to(lanes_v[NNZ + j:NNZ + j + 1, lanes], (16, 128))
            picks.append(jnp.where(held, pick, -1.0).astype(BF16))
        one = jnp.ones((16, 128), BF16)
        zero = jnp.zeros((16, 128), BF16)
        for b in range(NB):
            hits = [jnp.where(pick == jnp.asarray(b, BF16), one, zero) for pick in picks]
            while len(hits) > 1:
                hits = [hits[n] + hits[n + 1] for n in range(0, len(hits), 2)]
            counts[pl.ds(pl.multiple_of(b * 128 + kc * 16, 16), 16), lanes] = hits[0]

    for run in range(RUNS):
        vol_copies[run].wait_recv()
        for z in range(2):
            for c in range(2):
                at = pl.ds(run * RUN * 8 + 4 + c * 2 + z, RUN, stride=8)
                vol_rows[at, :] = vol_recv[run, z * 2 + c].astype(F32)
        vol_low = vol_rows[run * RUN * 8:(run + 1) * RUN * 8, :].astype(BF16)

        @pl.loop(0, NB // 8)
        def _(step, run=run, vol_low=vol_low):
            cols = pl.ds(pl.multiple_of(step * 1024, 1024), 1024)
            out = jnp.dot(vol_low, foot_wide[:, cols], preferred_element_type=F32)
            for n in range(8):
                bank[pl.ds((step * 8 + n) * KT + run * RUN, RUN)] = (
                    out[:, n * 128:(n + 1) * 128].reshape(RUN, 8, 128)
                )

    first_copy = remote(vol_send.at[:, pl.ds(0, 2)], first_recv, RUNS, down_id)
    first_copy.start()

    local[2].wait()
    local[3].wait()
    for c in range(2):
        term = plane(tvd_v, c, 1) / penalty_tv - plane(split_v, c, 1) - plane(vol_v, c, 1)
        last_send[c] = term.astype(BF16)
    last_copy = remote(last_send, last_recv, RUNS + 1, up_id)
    last_copy.start()

    bank[DEAD] = jnp.zeros((8, 128), F32)

    codes_copy.wait()

    def project(px, pw):
        peer = px * 8 + pw
        for row in range(ROWS):
            angle = px * 32 + half * 16 + pw * 2 + row // RAYS
            got = [bank[codes[row % RAYS * NNZ + j, angle]] for j in range(NNZ)]
            while len(got) > 1:
                got = [got[n] + got[n + 1] for n in range(0, len(got), 2)]
            ray_rows[row * 8:(row + 1) * 8, :] = got[0]
        proj_send[peer] = ray_rows[...].astype(BF16)
        rows = pl.ds(pl.multiple_of(peer * ROWS, ROWS), ROWS)
        for part in range(2):
            for c in range(2):
                for z in range(2):
                    at = z * 2 + c
                    plane_rows = ray_rows[pl.ds(part * 4 + c * 2 + z, ROWS, stride=8), :]
                    resid[part, rows, at * 128:(at + 1) * 128] = plane_rows.astype(BF16)

    @pl.loop(1, PEERS)
    def _(i):
        px, pw = peer_of(i)
        project(px, pw)
        exchange(proj_send, proj_recv, proj_ssem, proj_rsem, px, pw).start()

    project(xi, wi)
    proj_recv[me] = proj_send[me]

    def subtract(px, pw):
        peer = px * 8 + pw
        rows = pl.ds(pl.multiple_of(peer * ROWS, ROWS), ROWS)
        for cz in range(8):
            cols = slice(cz % 4 * 128, (cz % 4 + 1) * 128)
            gap = resid[cz // 4, rows, cols].astype(F32) - meas_recv[peer, cz].astype(F32)
            resid[cz // 4, rows, cols] = gap.astype(BF16)

    subtract(xi, wi)

    @pl.loop(1, PEERS)
    def _(i):
        px, pw = peer_of(i)
        arrival(meas_send, meas_recv, meas_ssem, meas_rsem, px, pw).wait_recv()
        subtract(px, pw)

    def backward(part, planes):
        first, last = planes.start, planes.stop
        rows_at = (last - first) * 128

        @pl.loop(0, NB // TALL)
        def _(step):
            rows = pl.ds(pl.multiple_of(step * (TALL * KT), TALL * KT), TALL * KT)
            out = jnp.dot(
                counts[rows, :], resid[part, :, first * 128:last * 128],
                preferred_element_type=F32,
            ).astype(BF16)
            for n in range(TALL):
                cols = pl.ds(pl.multiple_of((step * TALL + n) * 128, 128), 128)
                for p in range(last - first):
                    grouped[p * 128:(p + 1) * 128, cols] = (
                        out[n * 128:(n + 1) * 128, p * 128:(p + 1) * 128]
                    )
        return lax.dot_general(
            grouped[:rows_at, :], foot_wide[...], (((1,), (1,)), ((), ())),
            preferred_element_type=F32,
        )

    part_copies = [
        remote(part_send.at[z], part_recv.at[z], RUNS + 2 + z, other) for z in range(2)
    ]
    for z in range(2):
        theirs = backward(1, slice(z * 2, z * 2 + 2))
        for c in range(2):
            part_send[z, c] = theirs[c * 128:(c + 1) * 128, :].astype(BF16)
        part_copies[z].start()
    back_own[...] = backward(0, slice(0, 4))

    row_at = lax.broadcasted_iota(jnp.int32, (KT, TILE_WIDTH), 0)
    col_at = lax.broadcasted_iota(jnp.int32, (KT, TILE_WIDTH), 1)
    inner_row = row_at < KT - 1
    inner_col = col_at < TILE_WIDTH - 1

    def along(image, axis):
        step = pltpu.roll(image, 127, axis) - image
        return jnp.where(inner_row if axis == 0 else inner_col, step, 0.0)

    def spread(part, axis):
        part = jnp.where(inner_row if axis == 0 else inner_col, part, 0.0)
        return pltpu.roll(part, 1, axis) - part

    def force(i, c, z):
        return plane(tvd_v, i * 2 + c, z) / penalty_tv - plane(split_v, i * 2 + c, z)

    first_copy.wait_recv()
    last_copy.wait_recv()
    for c in range(2):
        images = [plane(vol_v, c, z) for z in range(2)]
        below = (last_recv[c].astype(F32) + images[0]) * keep_below
        middle = images[1] - images[0] + force(0, c, 0)
        above = (first_recv[:, c].reshape(KT, 128).astype(F32) - images[1] + force(0, c, 1)) * keep
        for z, slices in enumerate((below - middle, middle - above)):
            total = slices
            for axis in range(2):
                total = total + spread(along(images[z], axis) + force(1 + axis, c, z), axis)
            adj_v[z * 2 + c] = penalty_tv * total

    for z in range(2):
        part_copies[z].wait_recv()
        for c in range(2):
            cz = z * 2 + c
            descent = back_own[cz * 128:(cz + 1) * 128, :] + part_recv[z, c].astype(F32) + adj_v[cz]
            image = plane(vol_v, c, z) - step_size * descent
            vol_v[pl.ds(c * 256 + z, KT, stride=2), :] = image
            if z == 0:
                next_send[c] = image.astype(BF16)
        if z == 0:
            next_copy = remote(next_send, next_recv, RUNS + 4, down_id)
            next_copy.start()
    vol_done = pltpu.make_async_copy(vol_v, vol_out, out_sem.at[0])
    vol_done.start()

    local[5].wait()

    @pl.loop(1, PEERS)
    def _(i):
        px, pw = peer_of(i)
        arrival(proj_send, proj_recv, proj_ssem, proj_rsem, px, pw).wait_recv()

    pair = lax.broadcasted_iota(jnp.int32, (8, 128), 0) // 2

    def one_of(pieces):
        low = jnp.where(pair == 0, pieces[0], pieces[1])
        high = jnp.where(pair == 2, pieces[2], pieces[3])
        return jnp.where(pair < 2, low, high)

    @pl.loop(0, PEERS // 4)
    def _(block):
        for two in range(ROWS // 2):
            wide = [
                proj_recv[block * 4 + n, two * 16:(two + 1) * 16, :].astype(F32) for n in range(4)
            ]
            for row in range(2):
                given = [tile[row * 8:(row + 1) * 8, :] for tile in wide]
                turned = [one_of([given[(g + d) % 4] for g in range(4)]) for d in range(4)]
                turned = [turned[0]] + [pltpu.roll(turned[d], 2 * d, 0) for d in range(1, 4)]
                for part in range(2):
                    for c in range(2):
                        g = part * 2 + c
                        proj = one_of([turned[(n - g) % 4] for n in range(4)])
                        at = (two * 2 + row) * 256 + c * 128 + block // 2 * 32 + block % 2 * 8
                        rows = pl.ds(pl.multiple_of(at + (half + part) % 2 * 16, 8), 8)
                        dual_v[rows, :] = 0.5 * (proj + dual_v[rows, :] - meas_v[rows, :])

    fit_done = pltpu.make_async_copy(dual_v, fit_out, out_sem.at[1])
    fit_done.start()

    for z in range(2):
        if z == 1:
            next_copy.wait_recv()
        for c in range(2):
            image = plane(vol_v, c, z)
            if z == 0:
                slices = plane(vol_v, c, 1) - image
            else:
                slices = (next_recv[c].astype(F32) - image) * keep
            steps = (slices, along(image, 0), along(image, 1))
            for i in range(3):
                rows = pl.ds((i * 2 + c) * 256 + z, KT, stride=2)
                dual = tvd_v[rows, :]
                arg = steps[i] + dual / penalty_tv
                bound = tv_weight / penalty_tv
                split = arg - jnp.clip(arg, -bound, bound)
                split_v[rows, :] = split
                tvd_v[rows, :] = dual + penalty_tv * (steps[i] - split)
    split_done = pltpu.make_async_copy(split_v, split_out, out_sem.at[2])
    split_done.start()
    tvd_done = pltpu.make_async_copy(tvd_v, tvd_out, out_sem.at[3])
    tvd_done.start()

    for copy in (*vol_copies, first_copy, last_copy, *part_copies, next_copy):
        copy.wait_send()

    @pl.loop(1, PEERS)
    def _(i):
        px, pw = peer_of(i)
        exchange(meas_send, meas_recv, meas_ssem, meas_rsem, px, pw).wait_send()
        exchange(proj_send, proj_recv, proj_ssem, proj_rsem, px, pw).wait_send()

    for copy in (vol_done, fit_done, split_done, tvd_done):
        copy.wait()


def hand_on(*refs):
    given, out, held = refs[:4], refs[4:8], refs[8:12]
    sems = refs[12]
    fetches = [pltpu.make_async_copy(given[n], held[n], sems.at[n]) for n in range(4)]
    stores = [pltpu.make_async_copy(held[n], out[n], sems.at[4 + n]) for n in range(4)]
    for copy in fetches:
        copy.start()
    for fetch, store in zip(fetches, stores):
        fetch.wait()
        store.start()
    for copy in stores:
        copy.wait()


def to_rows(array):
    lead = array.shape[:-2]
    tiles = array.reshape(*lead, 2, KT, TILE_WIDTH)
    return jnp.swapaxes(tiles, -3, -2).reshape(-1, TILE_WIDTH)


def from_rows(rows, shape):
    tiles = rows.reshape(*shape[:-2], KT, 2, TILE_WIDTH)
    return jnp.swapaxes(tiles, -3, -2).reshape(shape)


def shards(
    volume, tv_split, tv_dual, measured, fit_dual, footprints, voxel_tile, kernel_pick, tile_count
):
    lists = [array.transpose(1, 2, 0).reshape(-1, 128) for array in (voxel_tile, kernel_pick)]

    hbm = pl.BlockSpec(memory_space=pl.ANY)
    vmem = pl.BlockSpec(memory_space=pltpu.VMEM)
    tile = (KT, TILE_WIDTH)
    result = [
        jax.ShapeDtypeStruct((512, 128), F32),
        jax.ShapeDtypeStruct((1536, 128), F32),
        jax.ShapeDtypeStruct((1536, 128), F32),
        jax.ShapeDtypeStruct((4096, 128), F32),
    ]
    held = pl.pallas_call(
        kernel,
        out_shape=result,
        in_specs=[vmem] * 3 + [hbm] * 6,
        out_specs=[hbm] * 4,
        scratch_shapes=[
            pltpu.VMEM((512, 128), F32),
            pltpu.VMEM((1536, 128), F32),
            pltpu.VMEM((1536, 128), F32),
            pltpu.VMEM((4096, 128), F32),
            pltpu.VMEM((4096, 128), F32),
            pltpu.VMEM((NB, 128, 128), BF16),
            pltpu.VMEM((128, NB * 128), BF16),
            pltpu.VMEM((RUNS, PLANES, RUN, 128), BF16),
            pltpu.VMEM((RUNS, PLANES, RUN, 128), BF16),
            pltpu.VMEM((1024, 128), F32),
            pltpu.VMEM((NB * KT + 8, 8, 128), F32),
            pltpu.VMEM((NB * KT, ALL_ROWS), BF16),
            pltpu.VMEM((512, NB * 128), BF16),
            pltpu.VMEM((PEERS, 8, ROWS, 128), BF16),
            pltpu.VMEM((PEERS, 8, ROWS, 128), BF16),
            pltpu.VMEM((PEERS, ROWS * 8, 128), BF16),
            pltpu.VMEM((PEERS, ROWS * 8, 128), BF16),
            pltpu.VMEM((2, ALL_ROWS, 512), BF16),
            pltpu.VMEM((ROWS * 8, 128), F32),
            pltpu.VMEM((RUNS, 2, RUN, 128), BF16),
            pltpu.VMEM((2, *tile), BF16),
            pltpu.VMEM((2, *tile), BF16),
            pltpu.VMEM((2, 2, *tile), BF16),
            pltpu.VMEM((2, 2, *tile), BF16),
            pltpu.VMEM((512, 128), F32),
            pltpu.VMEM((PLANES, *tile), F32),
            pltpu.VMEM((2, *tile), BF16),
            pltpu.VMEM((2, *tile), BF16),
            pltpu.VMEM((RAYS * NNZ, 128), jnp.int32),
            pltpu.SMEM((RAYS * NNZ, 128), jnp.int32),
            pltpu.VMEM((2 * NNZ, ALL_ROWS), F32),
            pltpu.SemaphoreType.DMA((7,)),
            pltpu.SemaphoreType.DMA((4,)),
            pltpu.SemaphoreType.DMA((PEERS,)),
            pltpu.SemaphoreType.DMA((PEERS,)),
            pltpu.SemaphoreType.DMA((PEERS,)),
            pltpu.SemaphoreType.DMA((PEERS,)),
            pltpu.SemaphoreType.DMA((RUNS + 5,)),
            pltpu.SemaphoreType.DMA((RUNS + 5,)),
        ],
        compiler_params=pltpu.CompilerParams(
            collective_id=0, has_side_effects=True, vmem_limit_bytes=60 * 1024 * 1024
        ),
    )(
        *lists, tile_count.T,
        to_rows(volume), to_rows(tv_split), to_rows(tv_dual),
        measured.reshape(4096, 128), fit_dual.reshape(4096, 128), footprints,
    )
    volume_next, split_next, tv_dual_next, fit_dual_next = pl.pallas_call(
        hand_on,
        out_shape=result,
        in_specs=[hbm] * 4,
        out_specs=[hbm] * 4,
        scratch_shapes=[
            *(pltpu.VMEM(leaf.shape, F32) for leaf in result),
            pltpu.SemaphoreType.DMA((8,)),
        ],
    )(*held)
    return (
        from_rows(volume_next, volume.shape),
        from_rows(split_next, tv_split.shape),
        from_rows(tv_dual_next, tv_dual.shape),
        fit_dual_next.reshape(fit_dual.shape),
    )


def solution(mesh):
    return jax.shard_map(
        shards,
        mesh=mesh,
        in_specs=(
            P(None, ("ang", "slab"), None),
            P(None, None, ("ang", "slab"), None),
            P(None, None, ("ang", "slab"), None),
            P("ang", None, None, None, "slab", None),
            P("ang", None, None, None, "slab", None),
            P(),
            P(),
            P(),
            P(),
        ),
        out_specs=(
            P(None, ("ang", "slab"), None),
            P(None, None, ("ang", "slab"), None),
            P(None, None, ("ang", "slab"), None),
            P("ang", None, None, None, "slab", None),
        ),
        check_vma=False,
    )
```

```python
import jax
import jax.numpy as jnp
from jax import lax
from jax.experimental import pallas as pl
from jax.experimental.pallas import tpu as pltpu
from jax.sharding import PartitionSpec as P

TILE_WIDTH = 128
VOLUME_CHANNELS = 2
KT = 128
NB = 40
NNZ = 8
RAYS = 8
PEERS = 32
ROWS = 16
PLANES = 4
ALL_ROWS = PEERS * ROWS
DEAD = NB * KT
WORDS = NB // 8
RUNS = 4
RUN = KT // RUNS
TALL = 8

penalty_tv = 0.5
tv_weight = 0.3
step_size = 0.3

F32 = jnp.float32
BF16 = jnp.bfloat16
MESH = pl.DeviceIdType.MESH


def kernel(
    tile_ref, pick_ref, live_ref, vol_hbm, split_hbm, tvd_hbm, meas_hbm, dual_hbm, foot_hbm,
    vol_v, split_v, tvd_v, dual_v,
    meas_v, foot_v,
    foot_wide, vol_send, vol_recv, vol_rows, bank, counts, grouped,
    meas_send, meas_recv, proj_send, proj_recv, resid, ray_rows,
    first_recv, last_send, last_recv, part_send, part_recv, back_own, adj_v,
    next_send, next_recv, code_v, codes, lanes_v, units_v,
    local_sem, meas_ssem, meas_rsem, proj_ssem, proj_rsem, one_ssem, one_rsem,
):
    ang = lax.axis_index("ang")
    slab = lax.axis_index("slab")
    xi = ang // 16
    half = (ang // 8) % 2
    wi = ang % 8
    yi = wi // 2
    core = wi % 2
    me = xi * 8 + wi
    other = (xi * 16 + (1 - half) * 8 + wi, slab)
    pos = ang * 4 + slab
    up = (pos + 1) % 256
    down = (pos + 255) % 256
    up_id = (up // 4, up % 4)
    down_id = (down // 4, down % 4)
    keep = (pos < 255).astype(F32)
    keep_below = (pos > 0).astype(F32)

    def peer_of(i):
        n = i % 16
        px = (xi + 4 - n % 4) % 4
        py = (yi + 8 - n % 4 - n // 4) % 4
        pc = (core + i // 16) % 2
        return px, py * 2 + pc

    def far_peer(i):
        px = (xi + 6 - i // 8) % 4
        py = (yi + 6 - i // 2 % 4) % 4
        return px, py * 2 + i % 2

    def ang_of(px, pw):
        return px * 16 + half * 8 + pw

    local = [
        pltpu.make_async_copy(vol_hbm, vol_v, local_sem.at[0]),
        pltpu.make_async_copy(meas_hbm, meas_v, local_sem.at[1]),
        pltpu.make_async_copy(split_hbm, split_v, local_sem.at[2]),
        pltpu.make_async_copy(tvd_hbm, tvd_v, local_sem.at[3]),
        pltpu.make_async_copy(foot_hbm, foot_v, local_sem.at[4]),
        pltpu.make_async_copy(dual_hbm, dual_v, local_sem.at[5]),
    ]
    for copy in local:
        copy.start()

    barrier = pltpu.get_barrier_semaphore()

    pl.semaphore_signal(barrier, inc=1, device_id=other, device_id_type=MESH)

    @pl.loop(0, PEERS)
    def _(i):
        px, pw = far_peer(i)

        @pl.when(px * 8 + pw != me)
        def _():
            pl.semaphore_signal(
                barrier, inc=1, device_id=(ang_of(px, pw), slab), device_id_type=MESH
            )

    for device in (up_id, down_id):
        pl.semaphore_signal(barrier, inc=1, device_id=device, device_id_type=MESH)

    def plane(ref, lead, z):
        return ref[pl.ds(lead * 256 + z, KT, stride=2), :]

    local[0].wait()
    for z in range(2):
        for c in range(2):
            cz = z * 2 + c
            image = plane(vol_v, c, z)
            vol_rows[pl.ds(c * 2 + z, KT, stride=8), :] = image
            for run in range(RUNS):
                vol_send[run, cz] = image[run * RUN:(run + 1) * RUN, :].astype(BF16)

    local[1].wait()

    def slice_row(px, pw, part, z, c):
        zh = px * 16 + ((half + part) % 2) * 8 + pw
        return c * 128 + zh * 2 + z

    def message(px, pw):
        peer = px * 8 + pw
        for part in range(2):
            for z in range(2):
                for c in range(2):
                    start = slice_row(px, pw, part, z, c)
                    rows = meas_v[pl.ds(start, ROWS, stride=256), :]
                    meas_send[peer, part * 4 + z * 2 + c] = rows.astype(BF16)

    @pl.loop(0, PEERS)
    def _(peer):
        message(peer // 8, peer % 8)

    for cz in range(8):
        meas_recv[me, cz] = meas_send[me, cz]

    def exchange(send, recv, ssem, rsem, px, pw):
        return pltpu.make_async_remote_copy(
            src_ref=send.at[px * 8 + pw], dst_ref=recv.at[me],
            send_sem=ssem.at[px * 8 + pw], recv_sem=rsem.at[me],
            device_id=(ang_of(px, pw), slab), device_id_type=MESH,
        )

    def arrival(send, recv, ssem, rsem, px, pw):
        return pltpu.make_async_remote_copy(
            src_ref=send.at[px * 8 + pw], dst_ref=recv.at[px * 8 + pw],
            send_sem=ssem.at[px * 8 + pw], recv_sem=rsem.at[px * 8 + pw],
            device_id=(ang_of(px, pw), slab), device_id_type=MESH,
        )

    entry_at = lax.broadcasted_iota(jnp.int32, (NNZ, 128), 0)
    lane = lax.broadcasted_iota(jnp.int32, (128, ALL_ROWS), 1)
    angle_at = lax.broadcasted_iota(jnp.int32, (128, ALL_ROWS), 0)
    peer_at = lane // ROWS
    wanted = peer_at // 8 * 32 + half * 16 + peer_at % 8 * 2 + lane // RAYS % 2
    same_angle = wanted == angle_at
    found = jnp.zeros((2 * NNZ, ALL_ROWS), F32)
    for r in range(RAYS):
        rows = slice(r * NNZ, (r + 1) * NNZ)
        is_live = entry_at < live_ref[r:r + 1, :]
        tiles = tile_ref[rows, :]
        picks = jnp.where(is_live, pick_ref[rows, :], NB)
        code_v[rows, :] = jnp.where(is_live, picks * KT + tiles, DEAD)
        both = jnp.concatenate([tiles, picks], axis=0).astype(F32).astype(BF16)
        chosen = jnp.where(same_angle & (lane % RAYS == r), 1.0, 0.0).astype(BF16)
        found = found + jnp.dot(both, chosen, preferred_element_type=F32)
    lanes_v[...] = found
    codes_copy = pltpu.make_async_copy(code_v, codes, local_sem.at[6])
    codes_copy.start()

    local[4].wait()
    for b in range(NB):
        foot_wide[:, b * 128:(b + 1) * 128] = foot_v[b]

    row_at = lax.broadcasted_iota(jnp.int32, (KT, TILE_WIDTH), 0)
    col_at = lax.broadcasted_iota(jnp.int32, (KT, TILE_WIDTH), 1)
    inner_row = row_at < KT - 1
    inner_col = col_at < TILE_WIDTH - 1

    def along(image, axis):
        step = pltpu.roll(image, 127, axis) - image
        return jnp.where(inner_row if axis == 0 else inner_col, step, 0.0)

    def spread(part, axis):
        part = jnp.where(inner_row if axis == 0 else inner_col, part, 0.0)
        return pltpu.roll(part, 1, axis) - part

    def force(i, c, z):
        return plane(tvd_v, i * 2 + c, z) / penalty_tv - plane(split_v, i * 2 + c, z)

    local[2].wait()
    local[3].wait()
    for c in range(2):
        images = [plane(vol_v, c, z) for z in range(2)]
        middle = images[1] - images[0] + force(0, c, 0)
        above = force(0, c, 1) - images[1]
        last_send[c] = above.astype(BF16)
        for z, slices in enumerate((-middle, middle - above * keep)):
            total = slices
            for axis in range(2):
                total = total + spread(along(images[z], axis) + force(1 + axis, c, z), axis)
            adj_v[z * 2 + c] = penalty_tv * total

    local[5].wait()

    @pl.loop(0, ROWS)
    def _(row):
        rows = pl.ds(pl.multiple_of(row * 256, 256), 256)
        dual_v[rows, :] = 0.5 * (dual_v[rows, :] - meas_v[rows, :])

    pl.semaphore_wait(barrier, PEERS + 2)

    def remote(src, dst, slot, device):
        return pltpu.make_async_remote_copy(
            src_ref=src, dst_ref=dst, send_sem=one_ssem.at[slot], recv_sem=one_rsem.at[slot],
            device_id=device, device_id_type=MESH,
        )

    vol_copies = [
        remote(vol_send.at[run], vol_recv.at[run], run, other) for run in range(RUNS)
    ]
    for copy in vol_copies:
        copy.start()

    @pl.loop(1, PEERS)
    def _(i):
        px, pw = peer_of(i)
        exchange(meas_send, meas_recv, meas_ssem, meas_rsem, px, pw).start()

    kernels = lanes_v[NNZ:2 * NNZ, :].astype(jnp.int32)
    unit = jnp.left_shift(1, (kernels & 7) * 4)
    for word in range(WORDS):
        units_v[word] = jnp.where(jnp.right_shift(kernels, 3) == word, unit, 0)

    @pl.loop(0, 32)
    def _(step):
        kc = step // 4
        lt = step % 4
        lanes = pl.ds(pl.multiple_of(lt * 128, 128), 128)
        tile = (lax.broadcasted_iota(jnp.int32, (16, 128), 0) + kc * 16).astype(F32)
        here = [
            jnp.broadcast_to(lanes_v[j:j + 1, lanes], (16, 128)) == tile for j in range(NNZ)
        ]
        for word in range(WORDS):
            total = None
            for j in range(NNZ):
                add = jnp.broadcast_to(units_v[word, j:j + 1, lanes], (16, 128))
                add = jnp.where(here[j], add, 0)
                total = add if total is None else total + add
            for n in range(8):
                count = lax.shift_right_logical(total, jnp.int32(4 * n)) & 15
                at = pl.multiple_of((word * 8 + n) * 128 + kc * 16, 16)
                counts[pl.ds(at, 16), lanes] = count.astype(F32).astype(BF16)

    for run in range(RUNS):
        vol_copies[run].wait_recv()
        for z in range(2):
            for c in range(2):
                at = pl.ds(run * RUN * 8 + 4 + c * 2 + z, RUN, stride=8)
                vol_rows[at, :] = vol_recv[run, z * 2 + c].astype(F32)
        vol_low = vol_rows[run * RUN * 8:(run + 1) * RUN * 8, :].astype(BF16)

        @pl.loop(0, NB // 8)
        def _(step, run=run, vol_low=vol_low):
            cols = pl.ds(pl.multiple_of(step * 1024, 1024), 1024)
            out = jnp.dot(vol_low, foot_wide[:, cols], preferred_element_type=F32)
            for n in range(8):
                bank[pl.ds((step * 8 + n) * KT + run * RUN, RUN)] = (
                    out[:, n * 128:(n + 1) * 128].reshape(RUN, 8, 128)
                )

    first_copy = remote(vol_send.at[:, pl.ds(0, 2)], first_recv, RUNS, down_id)
    first_copy.start()

    last_copy = remote(last_send, last_recv, RUNS + 1, up_id)
    last_copy.start()

    bank[DEAD] = jnp.zeros((8, 128), F32)

    codes_copy.wait()

    def project(px, pw):
        peer = px * 8 + pw
        for row in range(ROWS):
            angle = px * 32 + half * 16 + pw * 2 + row // RAYS
            got = [bank[codes[row % RAYS * NNZ + j, angle]] for j in range(NNZ)]
            while len(got) > 1:
                got = [got[n] + got[n + 1] for n in range(0, len(got), 2)]
            ray_rows[row * 8:(row + 1) * 8, :] = got[0]
        proj_send[peer] = ray_rows[...].astype(BF16)
        rows = pl.ds(pl.multiple_of(peer * ROWS, ROWS), ROWS)
        for part in range(2):
            for c in range(2):
                for z in range(2):
                    at = z * 2 + c
                    plane_rows = ray_rows[pl.ds(part * 4 + c * 2 + z, ROWS, stride=8), :]
                    resid[part, rows, at * 128:(at + 1) * 128] = plane_rows.astype(BF16)

    @pl.loop(1, PEERS)
    def _(i):
        px, pw = peer_of(i)
        project(px, pw)
        exchange(proj_send, proj_recv, proj_ssem, proj_rsem, px, pw).start()

    project(xi, wi)
    proj_recv[me] = proj_send[me]

    def subtract(px, pw):
        peer = px * 8 + pw
        rows = pl.ds(pl.multiple_of(peer * ROWS, ROWS), ROWS)
        for cz in range(8):
            cols = slice(cz % 4 * 128, (cz % 4 + 1) * 128)
            gap = resid[cz // 4, rows, cols].astype(F32) - meas_recv[peer, cz].astype(F32)
            resid[cz // 4, rows, cols] = gap.astype(BF16)

    subtract(xi, wi)

    @pl.loop(1, PEERS)
    def _(i):
        px, pw = peer_of(i)
        arrival(meas_send, meas_recv, meas_ssem, meas_rsem, px, pw).wait_recv()
        subtract(px, pw)

    def backward(part, planes):
        first, last = planes.start, planes.stop
        rows_at = (last - first) * 128

        @pl.loop(0, NB // TALL)
        def _(step):
            rows = pl.ds(pl.multiple_of(step * (TALL * KT), TALL * KT), TALL * KT)
            out = jnp.dot(
                counts[rows, :], resid[part, :, first * 128:last * 128],
                preferred_element_type=F32,
            ).astype(BF16)
            for n in range(TALL):
                cols = pl.ds(pl.multiple_of((step * TALL + n) * 128, 128), 128)
                for p in range(last - first):
                    grouped[p * 128:(p + 1) * 128, cols] = (
                        out[n * 128:(n + 1) * 128, p * 128:(p + 1) * 128]
                    )
        return lax.dot_general(
            grouped[:rows_at, :], foot_wide[...], (((1,), (1,)), ((), ())),
            preferred_element_type=F32,
        )

    part_copies = [
        remote(part_send.at[z], part_recv.at[z], RUNS + 2 + z, other) for z in range(2)
    ]
    for z in range(2):
        theirs = backward(1, slice(z * 2, z * 2 + 2))
        for c in range(2):
            part_send[z, c] = theirs[c * 128:(c + 1) * 128, :].astype(BF16)
        part_copies[z].start()
    back_own[...] = backward(0, slice(0, 4))

    first_copy.wait_recv()
    last_copy.wait_recv()
    for z in range(2):
        part_copies[z].wait_recv()
        for c in range(2):
            cz = z * 2 + c
            image = plane(vol_v, c, z)
            if z == 0:
                slices = (last_recv[c].astype(F32) + image) * keep_below
            else:
                slices = first_recv[:, c].reshape(KT, 128).astype(F32) * -keep
            descent = (
                back_own[cz * 128:(cz + 1) * 128, :] + part_recv[z, c].astype(F32)
                + (adj_v[cz] + penalty_tv * slices)
            )
            image = image - step_size * descent
            vol_v[pl.ds(c * 256 + z, KT, stride=2), :] = image
            if z == 0:
                next_send[c] = image.astype(BF16)
        if z == 0:
            next_copy = remote(next_send, next_recv, RUNS + 4, down_id)
            next_copy.start()

    @pl.loop(1, PEERS)
    def _(i):
        px, pw = peer_of(i)
        arrival(proj_send, proj_recv, proj_ssem, proj_rsem, px, pw).wait_recv()

    pair = lax.broadcasted_iota(jnp.int32, (8, 128), 0) // 2

    def one_of(pieces):
        low = jnp.where(pair == 0, pieces[0], pieces[1])
        high = jnp.where(pair == 2, pieces[2], pieces[3])
        return jnp.where(pair < 2, low, high)

    @pl.loop(0, PEERS // 4)
    def _(block):
        for two in range(ROWS // 2):
            wide = [
                proj_recv[block * 4 + n, two * 16:(two + 1) * 16, :].astype(F32) for n in range(4)
            ]
            for row in range(2):
                given = [tile[row * 8:(row + 1) * 8, :] for tile in wide]
                turned = [one_of([given[(g + d) % 4] for g in range(4)]) for d in range(4)]
                turned = [turned[0]] + [pltpu.roll(turned[d], 2 * d, 0) for d in range(1, 4)]
                for part in range(2):
                    for c in range(2):
                        g = part * 2 + c
                        proj = one_of([turned[(n - g) % 4] for n in range(4)])
                        at = (two * 2 + row) * 256 + c * 128 + block // 2 * 32 + block % 2 * 8
                        rows = pl.ds(pl.multiple_of(at + (half + part) % 2 * 16, 8), 8)
                        dual_v[rows, :] = dual_v[rows, :] + 0.5 * proj

    for z in range(2):
        if z == 1:
            next_copy.wait_recv()
        for c in range(2):
            image = plane(vol_v, c, z)
            if z == 0:
                slices = plane(vol_v, c, 1) - image
            else:
                slices = (next_recv[c].astype(F32) - image) * keep
            steps = (slices, along(image, 0), along(image, 1))
            for i in range(3):
                rows = pl.ds((i * 2 + c) * 256 + z, KT, stride=2)
                dual = tvd_v[rows, :]
                arg = steps[i] + dual / penalty_tv
                bound = tv_weight / penalty_tv
                split = arg - jnp.clip(arg, -bound, bound)
                split_v[rows, :] = split
                tvd_v[rows, :] = dual + penalty_tv * (steps[i] - split)

    for copy in (*vol_copies, first_copy, last_copy, *part_copies, next_copy):
        copy.wait_send()

    @pl.loop(1, PEERS)
    def _(i):
        px, pw = peer_of(i)
        exchange(meas_send, meas_recv, meas_ssem, meas_rsem, px, pw).wait_send()
        exchange(proj_send, proj_recv, proj_ssem, proj_rsem, px, pw).wait_send()


def hand_on(*refs):
    copies = [pltpu.make_async_copy(refs[n], refs[4 + n], refs[8].at[n]) for n in range(4)]
    for copy in copies:
        copy.start()
    for copy in copies:
        copy.wait()


def to_rows(array):
    lead = array.shape[:-2]
    tiles = array.reshape(*lead, 2, KT, TILE_WIDTH)
    return jnp.swapaxes(tiles, -3, -2).reshape(-1, TILE_WIDTH)


def from_rows(rows, shape):
    tiles = rows.reshape(*shape[:-2], KT, 2, TILE_WIDTH)
    return jnp.swapaxes(tiles, -3, -2).reshape(shape)


def shards(
    volume, tv_split, tv_dual, measured, fit_dual, footprints, voxel_tile, kernel_pick, tile_count
):
    lists = [array.transpose(1, 2, 0).reshape(-1, 128) for array in (voxel_tile, kernel_pick)]

    hbm = pl.BlockSpec(memory_space=pl.ANY)
    vmem = pl.BlockSpec(memory_space=pltpu.VMEM)
    tile = (KT, TILE_WIDTH)
    result = [
        jax.ShapeDtypeStruct((512, 128), F32),
        jax.ShapeDtypeStruct((1536, 128), F32),
        jax.ShapeDtypeStruct((1536, 128), F32),
        jax.ShapeDtypeStruct((4096, 128), F32),
    ]
    held = pl.pallas_call(
        kernel,
        out_shape=[pltpu.VMEM(leaf.shape, F32) for leaf in result],
        in_specs=[vmem] * 3 + [hbm] * 6,
        out_specs=[vmem] * 4,
        scratch_shapes=[
            pltpu.VMEM((4096, 128), F32),
            pltpu.VMEM((NB, 128, 128), BF16),
            pltpu.VMEM((128, NB * 128), BF16),
            pltpu.VMEM((RUNS, PLANES, RUN, 128), BF16),
            pltpu.VMEM((RUNS, PLANES, RUN, 128), BF16),
            pltpu.VMEM((1024, 128), F32),
            pltpu.VMEM((NB * KT + 8, 8, 128), F32),
            pltpu.VMEM((NB * KT, ALL_ROWS), BF16),
            pltpu.VMEM((512, NB * 128), BF16),
            pltpu.VMEM((PEERS, 8, ROWS, 128), BF16),
            pltpu.VMEM((PEERS, 8, ROWS, 128), BF16),
            pltpu.VMEM((PEERS, ROWS * 8, 128), BF16),
            pltpu.VMEM((PEERS, ROWS * 8, 128), BF16),
            pltpu.VMEM((2, ALL_ROWS, 512), BF16),
            pltpu.VMEM((ROWS * 8, 128), F32),
            pltpu.VMEM((RUNS, 2, RUN, 128), BF16),
            pltpu.VMEM((2, *tile), BF16),
            pltpu.VMEM((2, *tile), BF16),
            pltpu.VMEM((2, 2, *tile), BF16),
            pltpu.VMEM((2, 2, *tile), BF16),
            pltpu.VMEM((512, 128), F32),
            pltpu.VMEM((PLANES, *tile), F32),
            pltpu.VMEM((2, *tile), BF16),
            pltpu.VMEM((2, *tile), BF16),
            pltpu.VMEM((RAYS * NNZ, 128), jnp.int32),
            pltpu.SMEM((RAYS * NNZ, 128), jnp.int32),
            pltpu.VMEM((2 * NNZ, ALL_ROWS), F32),
            pltpu.VMEM((WORDS, NNZ, ALL_ROWS), jnp.int32),
            pltpu.SemaphoreType.DMA((7,)),
            pltpu.SemaphoreType.DMA((PEERS,)),
            pltpu.SemaphoreType.DMA((PEERS,)),
            pltpu.SemaphoreType.DMA((PEERS,)),
            pltpu.SemaphoreType.DMA((PEERS,)),
            pltpu.SemaphoreType.DMA((RUNS + 5,)),
            pltpu.SemaphoreType.DMA((RUNS + 5,)),
        ],
        compiler_params=pltpu.CompilerParams(
            collective_id=0, has_side_effects=True, vmem_limit_bytes=52 * 1024 * 1024
        ),
    )(
        *lists, tile_count.T,
        to_rows(volume), to_rows(tv_split), to_rows(tv_dual),
        measured.reshape(4096, 128), fit_dual.reshape(4096, 128), footprints,
    )
    volume_next, split_next, tv_dual_next, fit_dual_next = pl.pallas_call(
        hand_on,
        out_shape=result,
        in_specs=[vmem] * 4,
        out_specs=[hbm] * 4,
        scratch_shapes=[pltpu.SemaphoreType.DMA((4,))],
        compiler_params=pltpu.CompilerParams(vmem_limit_bytes=2 * 1024 * 1024),
    )(*held)
    return (
        from_rows(volume_next, volume.shape),
        from_rows(split_next, tv_split.shape),
        from_rows(tv_dual_next, tv_dual.shape),
        fit_dual_next.reshape(fit_dual.shape),
    )


def solution(mesh):
    return jax.shard_map(
        shards,
        mesh=mesh,
        in_specs=(
            P(None, ("ang", "slab"), None),
            P(None, None, ("ang", "slab"), None),
            P(None, None, ("ang", "slab"), None),
            P("ang", None, None, None, "slab", None),
            P("ang", None, None, None, "slab", None),
            P(),
            P(),
            P(),
            P(),
        ),
        out_specs=(
            P(None, ("ang", "slab"), None),
            P(None, None, ("ang", "slab"), None),
            P(None, None, ("ang", "slab"), None),
            P("ang", None, None, None, "slab", None),
        ),
        check_vma=False,
    )
```

```python
import jax
import jax.numpy as jnp
from jax import lax
from jax.experimental import pallas as pl
from jax.experimental.pallas import tpu as pltpu
from jax.sharding import PartitionSpec as P

TILE_WIDTH = 128
VOLUME_CHANNELS = 2
KT = 128
NB = 40
NNZ = 8
RAYS = 8
PEERS = 32
ROWS = 16
PLANES = 4
ALL_ROWS = PEERS * ROWS
DEAD = NB * KT
WORDS = NB // 8
RUNS = 4
RUN = KT // RUNS
TALL = 20

penalty_tv = 0.5
tv_weight = 0.3
step_size = 0.3

F32 = jnp.float32
BF16 = jnp.bfloat16
MESH = pl.DeviceIdType.MESH


def kernel(
    tile_ref, pick_ref, live_ref, vol_hbm, split_hbm, tvd_hbm, meas_hbm, dual_hbm, foot_hbm,
    vol_v, split_v, tvd_v, dual_v,
    meas_v, foot_v,
    foot_wide, vol_send, vol_recv, vol_rows, bank, counts, grouped,
    meas_send, meas_recv, proj_send, proj_recv, resid, ray_rows,
    first_recv, last_send, last_recv, part_send, part_recv, back_own, adj_v,
    next_send, next_recv, code_v, codes, lanes_v, units_v,
    local_sem, meas_ssem, meas_rsem, proj_ssem, proj_rsem, one_ssem, one_rsem,
):
    ang = lax.axis_index("ang")
    slab = lax.axis_index("slab")
    xi = ang // 16
    half = (ang // 8) % 2
    wi = ang % 8
    yi = wi // 2
    core = wi % 2
    me = xi * 8 + wi
    other = (xi * 16 + (1 - half) * 8 + wi, slab)
    pos = ang * 4 + slab
    up = (pos + 1) % 256
    down = (pos + 255) % 256
    up_id = (up // 4, up % 4)
    down_id = (down // 4, down % 4)
    keep = (pos < 255).astype(F32)
    keep_below = (pos > 0).astype(F32)

    def peer_of(i):
        n = i % 16
        px = (xi + 4 - n % 4) % 4
        py = (yi + 8 - n % 4 - n // 4) % 4
        pc = (core + i // 16) % 2
        return px, py * 2 + pc

    def far_peer(i):
        px = (xi + 6 - i // 8) % 4
        py = (yi + 6 - i // 2 % 4) % 4
        return px, py * 2 + i % 2

    def ang_of(px, pw):
        return px * 16 + half * 8 + pw

    local = [
        pltpu.make_async_copy(vol_hbm, vol_v, local_sem.at[0]),
        pltpu.make_async_copy(meas_hbm, meas_v, local_sem.at[1]),
        pltpu.make_async_copy(split_hbm, split_v, local_sem.at[2]),
        pltpu.make_async_copy(tvd_hbm, tvd_v, local_sem.at[3]),
        pltpu.make_async_copy(foot_hbm, foot_v, local_sem.at[4]),
        pltpu.make_async_copy(dual_hbm, dual_v, local_sem.at[5]),
    ]
    for copy in local:
        copy.start()

    barrier = pltpu.get_barrier_semaphore()

    pl.semaphore_signal(barrier, inc=1, device_id=other, device_id_type=MESH)

    @pl.loop(0, PEERS)
    def _(i):
        px, pw = far_peer(i)

        @pl.when(px * 8 + pw != me)
        def _():
            pl.semaphore_signal(
                barrier, inc=1, device_id=(ang_of(px, pw), slab), device_id_type=MESH
            )

    for device in (up_id, down_id):
        pl.semaphore_signal(barrier, inc=1, device_id=device, device_id_type=MESH)

    def plane(ref, lead, z):
        return ref[pl.ds(lead * 256 + z, KT, stride=2), :]

    local[0].wait()
    for z in range(2):
        for c in range(2):
            cz = z * 2 + c
            image = plane(vol_v, c, z)
            vol_rows[pl.ds(c * 2 + z, KT, stride=8), :] = image
            for run in range(RUNS):
                vol_send[run, cz] = image[run * RUN:(run + 1) * RUN, :].astype(BF16)

    local[1].wait()

    def slice_row(px, pw, part, z, c):
        zh = px * 16 + ((half + part) % 2) * 8 + pw
        return c * 128 + zh * 2 + z

    def message(px, pw):
        peer = px * 8 + pw
        for part in range(2):
            for z in range(2):
                for c in range(2):
                    start = slice_row(px, pw, part, z, c)
                    rows = meas_v[pl.ds(start, ROWS, stride=256), :]
                    meas_send[peer, part * 4 + z * 2 + c] = rows.astype(BF16)

    @pl.loop(0, PEERS)
    def _(peer):
        message(peer // 8, peer % 8)

    for cz in range(8):
        meas_recv[me, cz] = meas_send[me, cz]

    def exchange(send, recv, ssem, rsem, px, pw):
        return pltpu.make_async_remote_copy(
            src_ref=send.at[px * 8 + pw], dst_ref=recv.at[me],
            send_sem=ssem.at[px * 8 + pw], recv_sem=rsem.at[me],
            device_id=(ang_of(px, pw), slab), device_id_type=MESH,
        )

    def arrival(send, recv, ssem, rsem, px, pw):
        return pltpu.make_async_remote_copy(
            src_ref=send.at[px * 8 + pw], dst_ref=recv.at[px * 8 + pw],
            send_sem=ssem.at[px * 8 + pw], recv_sem=rsem.at[px * 8 + pw],
            device_id=(ang_of(px, pw), slab), device_id_type=MESH,
        )

    entry_at = lax.broadcasted_iota(jnp.int32, (NNZ, 128), 0)
    lane = lax.broadcasted_iota(jnp.int32, (128, ALL_ROWS), 1)
    angle_at = lax.broadcasted_iota(jnp.int32, (128, ALL_ROWS), 0)
    peer_at = lane // ROWS
    wanted = peer_at // 8 * 32 + half * 16 + peer_at % 8 * 2 + lane // RAYS % 2
    same_angle = wanted == angle_at
    found = jnp.zeros((2 * NNZ, ALL_ROWS), F32)
    for r in range(RAYS):
        rows = slice(r * NNZ, (r + 1) * NNZ)
        is_live = entry_at < live_ref[r:r + 1, :]
        tiles = tile_ref[rows, :]
        picks = jnp.where(is_live, pick_ref[rows, :], NB)
        code_v[rows, :] = jnp.where(is_live, picks * KT + tiles, DEAD)
        both = jnp.concatenate([tiles, picks], axis=0).astype(F32).astype(BF16)
        chosen = jnp.where(same_angle & (lane % RAYS == r), 1.0, 0.0).astype(BF16)
        found = found + jnp.dot(both, chosen, preferred_element_type=F32)
    lanes_v[...] = found
    codes_copy = pltpu.make_async_copy(code_v, codes, local_sem.at[6])
    codes_copy.start()

    local[4].wait()
    for b in range(NB):
        foot_wide[:, b * 128:(b + 1) * 128] = foot_v[b]

    row_at = lax.broadcasted_iota(jnp.int32, (KT, TILE_WIDTH), 0)
    col_at = lax.broadcasted_iota(jnp.int32, (KT, TILE_WIDTH), 1)
    inner_row = row_at < KT - 1
    inner_col = col_at < TILE_WIDTH - 1

    def along(image, axis):
        step = pltpu.roll(image, 127, axis) - image
        return jnp.where(inner_row if axis == 0 else inner_col, step, 0.0)

    def spread(part, axis):
        part = jnp.where(inner_row if axis == 0 else inner_col, part, 0.0)
        return pltpu.roll(part, 1, axis) - part

    def force(i, c, z):
        return plane(tvd_v, i * 2 + c, z) / penalty_tv - plane(split_v, i * 2 + c, z)

    local[2].wait()
    local[3].wait()
    for c in range(2):
        images = [plane(vol_v, c, z) for z in range(2)]
        middle = images[1] - images[0] + force(0, c, 0)
        above = force(0, c, 1) - images[1]
        last_send[c] = above.astype(BF16)
        for z, slices in enumerate((-middle, middle - above * keep)):
            total = slices
            for axis in range(2):
                total = total + spread(along(images[z], axis) + force(1 + axis, c, z), axis)
            adj_v[z * 2 + c] = penalty_tv * total

    local[5].wait()

    @pl.loop(0, ROWS)
    def _(row):
        rows = pl.ds(pl.multiple_of(row * 256, 256), 256)
        dual_v[rows, :] = 0.5 * (dual_v[rows, :] - meas_v[rows, :])

    pl.semaphore_wait(barrier, PEERS + 2)

    def remote(src, dst, slot, device):
        return pltpu.make_async_remote_copy(
            src_ref=src, dst_ref=dst, send_sem=one_ssem.at[slot], recv_sem=one_rsem.at[slot],
            device_id=device, device_id_type=MESH,
        )

    vol_copies = [
        remote(vol_send.at[run], vol_recv.at[run], run, other) for run in range(RUNS)
    ]
    for copy in vol_copies:
        copy.start()

    @pl.loop(1, PEERS)
    def _(i):
        px, pw = peer_of(i)
        exchange(meas_send, meas_recv, meas_ssem, meas_rsem, px, pw).start()

    kernels = lanes_v[NNZ:2 * NNZ, :].astype(jnp.int32)
    unit = jnp.left_shift(1, (kernels & 7) * 4)
    for word in range(WORDS):
        units_v[word] = jnp.where(jnp.right_shift(kernels, 3) == word, unit, 0)

    @pl.loop(0, 32)
    def _(step):
        kc = step // 4
        lt = step % 4
        lanes = pl.ds(pl.multiple_of(lt * 128, 128), 128)
        tile = (lax.broadcasted_iota(jnp.int32, (16, 128), 0) + kc * 16).astype(F32)
        here = [
            jnp.broadcast_to(lanes_v[j:j + 1, lanes], (16, 128)) == tile for j in range(NNZ)
        ]
        for word in range(WORDS):
            total = None
            for j in range(NNZ):
                add = jnp.broadcast_to(units_v[word, j:j + 1, lanes], (16, 128))
                add = jnp.where(here[j], add, 0)
                total = add if total is None else total + add
            for n in range(8):
                count = lax.shift_right_logical(total, jnp.int32(4 * n)) & 15
                at = pl.multiple_of((word * 8 + n) * 128 + kc * 16, 16)
                counts[pl.ds(at, 16), lanes] = count.astype(F32).astype(BF16)

    for run in range(RUNS):
        vol_copies[run].wait_recv()
        for z in range(2):
            for c in range(2):
                at = pl.ds(run * RUN * 8 + 4 + c * 2 + z, RUN, stride=8)
                vol_rows[at, :] = vol_recv[run, z * 2 + c].astype(F32)
        vol_low = vol_rows[run * RUN * 8:(run + 1) * RUN * 8, :].astype(BF16)

        @pl.loop(0, NB // 8)
        def _(step, run=run, vol_low=vol_low):
            cols = pl.ds(pl.multiple_of(step * 1024, 1024), 1024)
            out = jnp.dot(vol_low, foot_wide[:, cols], preferred_element_type=F32)
            for n in range(8):
                bank[pl.ds((step * 8 + n) * KT + run * RUN, RUN)] = (
                    out[:, n * 128:(n + 1) * 128].reshape(RUN, 8, 128)
                )

    first_copy = remote(vol_send.at[:, pl.ds(0, 2)], first_recv, RUNS, down_id)
    first_copy.start()

    last_copy = remote(last_send, last_recv, RUNS + 1, up_id)
    last_copy.start()

    bank[DEAD] = jnp.zeros((8, 128), F32)

    codes_copy.wait()

    def project(px, pw):
        peer = px * 8 + pw
        for row in range(ROWS):
            angle = px * 32 + half * 16 + pw * 2 + row // RAYS
            got = [bank[codes[row % RAYS * NNZ + j, angle]] for j in range(NNZ)]
            while len(got) > 1:
                got = [got[n] + got[n + 1] for n in range(0, len(got), 2)]
            ray_rows[row * 8:(row + 1) * 8, :] = got[0]
        proj_send[peer] = ray_rows[...].astype(BF16)
        rows = pl.ds(pl.multiple_of(peer * ROWS, ROWS), ROWS)
        for part in range(2):
            for c in range(2):
                for z in range(2):
                    at = z * 2 + c
                    plane_rows = ray_rows[pl.ds(part * 4 + c * 2 + z, ROWS, stride=8), :]
                    resid[part, rows, at * 128:(at + 1) * 128] = plane_rows.astype(BF16)

    @pl.loop(1, PEERS)
    def _(i):
        px, pw = peer_of(i)
        project(px, pw)
        exchange(proj_send, proj_recv, proj_ssem, proj_rsem, px, pw).start()

    project(xi, wi)
    proj_recv[me] = proj_send[me]

    def subtract(px, pw):
        peer = px * 8 + pw
        rows = pl.ds(pl.multiple_of(peer * ROWS, ROWS), ROWS)
        for cz in range(8):
            cols = slice(cz % 4 * 128, (cz % 4 + 1) * 128)
            gap = resid[cz // 4, rows, cols].astype(F32) - meas_recv[peer, cz].astype(F32)
            resid[cz // 4, rows, cols] = gap.astype(BF16)

    subtract(xi, wi)

    @pl.loop(1, PEERS)
    def _(i):
        px, pw = peer_of(i)
        arrival(meas_send, meas_recv, meas_ssem, meas_rsem, px, pw).wait_recv()
        subtract(px, pw)

    def backward(part, planes):
        first, last = planes.start, planes.stop
        rows_at = (last - first) * 128

        @pl.loop(0, NB // TALL)
        def _(step):
            rows = pl.ds(pl.multiple_of(step * (TALL * KT), TALL * KT), TALL * KT)
            out = jnp.dot(
                counts[rows, :], resid[part, :, first * 128:last * 128],
                preferred_element_type=F32,
            ).astype(BF16)
            for n in range(TALL):
                cols = pl.ds(pl.multiple_of((step * TALL + n) * 128, 128), 128)
                for p in range(last - first):
                    grouped[p * 128:(p + 1) * 128, cols] = (
                        out[n * 128:(n + 1) * 128, p * 128:(p + 1) * 128]
                    )
        return lax.dot_general(
            grouped[:rows_at, :], foot_wide[...], (((1,), (1,)), ((), ())),
            preferred_element_type=F32,
        )

    part_copies = [
        remote(part_send.at[z], part_recv.at[z], RUNS + 2 + z, other) for z in range(2)
    ]
    for z in range(2):
        theirs = backward(1, slice(z * 2, z * 2 + 2))
        for c in range(2):
            part_send[z, c] = theirs[c * 128:(c + 1) * 128, :].astype(BF16)
        part_copies[z].start()
    back_own[...] = backward(0, slice(0, 4))

    first_copy.wait_recv()
    last_copy.wait_recv()
    for z in range(2):
        part_copies[z].wait_recv()
        for c in range(2):
            cz = z * 2 + c
            image = plane(vol_v, c, z)
            if z == 0:
                slices = (last_recv[c].astype(F32) + image) * keep_below
            else:
                slices = first_recv[:, c].reshape(KT, 128).astype(F32) * -keep
            descent = (
                back_own[cz * 128:(cz + 1) * 128, :] + part_recv[z, c].astype(F32)
                + (adj_v[cz] + penalty_tv * slices)
            )
            image = image - step_size * descent
            vol_v[pl.ds(c * 256 + z, KT, stride=2), :] = image
            if z == 0:
                next_send[c] = image.astype(BF16)
        if z == 0:
            next_copy = remote(next_send, next_recv, RUNS + 4, down_id)
            next_copy.start()

    @pl.loop(1, PEERS)
    def _(i):
        px, pw = peer_of(i)
        arrival(proj_send, proj_recv, proj_ssem, proj_rsem, px, pw).wait_recv()

    pair = lax.broadcasted_iota(jnp.int32, (8, 128), 0) // 2

    def one_of(pieces):
        low = jnp.where(pair == 0, pieces[0], pieces[1])
        high = jnp.where(pair == 2, pieces[2], pieces[3])
        return jnp.where(pair < 2, low, high)

    @pl.loop(0, PEERS // 4)
    def _(block):
        for two in range(ROWS // 2):
            wide = [
                proj_recv[block * 4 + n, two * 16:(two + 1) * 16, :].astype(F32) for n in range(4)
            ]
            for row in range(2):
                given = [tile[row * 8:(row + 1) * 8, :] for tile in wide]
                turned = [one_of([given[(g + d) % 4] for g in range(4)]) for d in range(4)]
                turned = [turned[0]] + [pltpu.roll(turned[d], 2 * d, 0) for d in range(1, 4)]
                for part in range(2):
                    for c in range(2):
                        g = part * 2 + c
                        proj = one_of([turned[(n - g) % 4] for n in range(4)])
                        at = (two * 2 + row) * 256 + c * 128 + block // 2 * 32 + block % 2 * 8
                        rows = pl.ds(pl.multiple_of(at + (half + part) % 2 * 16, 8), 8)
                        dual_v[rows, :] = dual_v[rows, :] + 0.5 * proj

    for z in range(2):
        if z == 1:
            next_copy.wait_recv()
        for c in range(2):
            image = plane(vol_v, c, z)
            if z == 0:
                slices = plane(vol_v, c, 1) - image
            else:
                slices = (next_recv[c].astype(F32) - image) * keep
            steps = (slices, along(image, 0), along(image, 1))
            for i in range(3):
                rows = pl.ds((i * 2 + c) * 256 + z, KT, stride=2)
                dual = tvd_v[rows, :]
                arg = steps[i] + dual / penalty_tv
                bound = tv_weight / penalty_tv
                split = arg - jnp.clip(arg, -bound, bound)
                split_v[rows, :] = split
                tvd_v[rows, :] = dual + penalty_tv * (steps[i] - split)

    for copy in (*vol_copies, first_copy, last_copy, *part_copies, next_copy):
        copy.wait_send()

    @pl.loop(1, PEERS)
    def _(i):
        px, pw = peer_of(i)
        exchange(meas_send, meas_recv, meas_ssem, meas_rsem, px, pw).wait_send()
        exchange(proj_send, proj_recv, proj_ssem, proj_rsem, px, pw).wait_send()


def hand_on(*refs):
    copies = [pltpu.make_async_copy(refs[n], refs[4 + n], refs[8].at[n]) for n in range(4)]
    for copy in copies:
        copy.start()
    for copy in copies:
        copy.wait()


def to_rows(array):
    lead = array.shape[:-2]
    tiles = array.reshape(*lead, 2, KT, TILE_WIDTH)
    return jnp.swapaxes(tiles, -3, -2).reshape(-1, TILE_WIDTH)


def from_rows(rows, shape):
    tiles = rows.reshape(*shape[:-2], KT, 2, TILE_WIDTH)
    return jnp.swapaxes(tiles, -3, -2).reshape(shape)


def shards(
    volume, tv_split, tv_dual, measured, fit_dual, footprints, voxel_tile, kernel_pick, tile_count
):
    lists = [array.transpose(1, 2, 0).reshape(-1, 128) for array in (voxel_tile, kernel_pick)]

    hbm = pl.BlockSpec(memory_space=pl.ANY)
    vmem = pl.BlockSpec(memory_space=pltpu.VMEM)
    tile = (KT, TILE_WIDTH)
    result = [
        jax.ShapeDtypeStruct((512, 128), F32),
        jax.ShapeDtypeStruct((1536, 128), F32),
        jax.ShapeDtypeStruct((1536, 128), F32),
        jax.ShapeDtypeStruct((4096, 128), F32),
    ]
    held = pl.pallas_call(
        kernel,
        out_shape=[pltpu.VMEM(leaf.shape, F32) for leaf in result],
        in_specs=[vmem] * 3 + [hbm] * 6,
        out_specs=[vmem] * 4,
        scratch_shapes=[
            pltpu.VMEM((4096, 128), F32),
            pltpu.VMEM((NB, 128, 128), BF16),
            pltpu.VMEM((128, NB * 128), BF16),
            pltpu.VMEM((RUNS, PLANES, RUN, 128), BF16),
            pltpu.VMEM((RUNS, PLANES, RUN, 128), BF16),
            pltpu.VMEM((1024, 128), F32),
            pltpu.VMEM((NB * KT + 8, 8, 128), F32),
            pltpu.VMEM((NB * KT, ALL_ROWS), BF16),
            pltpu.VMEM((512, NB * 128), BF16),
            pltpu.VMEM((PEERS, 8, ROWS, 128), BF16),
            pltpu.VMEM((PEERS, 8, ROWS, 128), BF16),
            pltpu.VMEM((PEERS, ROWS * 8, 128), BF16),
            pltpu.VMEM((PEERS, ROWS * 8, 128), BF16),
            pltpu.VMEM((2, ALL_ROWS, 512), BF16),
            pltpu.VMEM((ROWS * 8, 128), F32),
            pltpu.VMEM((RUNS, 2, RUN, 128), BF16),
            pltpu.VMEM((2, *tile), BF16),
            pltpu.VMEM((2, *tile), BF16),
            pltpu.VMEM((2, 2, *tile), BF16),
            pltpu.VMEM((2, 2, *tile), BF16),
            pltpu.VMEM((512, 128), F32),
            pltpu.VMEM((PLANES, *tile), F32),
            pltpu.VMEM((2, *tile), BF16),
            pltpu.VMEM((2, *tile), BF16),
            pltpu.VMEM((RAYS * NNZ, 128), jnp.int32),
            pltpu.SMEM((RAYS * NNZ, 128), jnp.int32),
            pltpu.VMEM((2 * NNZ, ALL_ROWS), F32),
            pltpu.VMEM((WORDS, NNZ, ALL_ROWS), jnp.int32),
            pltpu.SemaphoreType.DMA((7,)),
            pltpu.SemaphoreType.DMA((PEERS,)),
            pltpu.SemaphoreType.DMA((PEERS,)),
            pltpu.SemaphoreType.DMA((PEERS,)),
            pltpu.SemaphoreType.DMA((PEERS,)),
            pltpu.SemaphoreType.DMA((RUNS + 5,)),
            pltpu.SemaphoreType.DMA((RUNS + 5,)),
        ],
        compiler_params=pltpu.CompilerParams(
            collective_id=0, has_side_effects=True, vmem_limit_bytes=52 * 1024 * 1024
        ),
    )(
        *lists, tile_count.T,
        to_rows(volume), to_rows(tv_split), to_rows(tv_dual),
        measured.reshape(4096, 128), fit_dual.reshape(4096, 128), footprints,
    )
    volume_next, split_next, tv_dual_next, fit_dual_next = pl.pallas_call(
        hand_on,
        out_shape=result,
        in_specs=[vmem] * 4,
        out_specs=[hbm] * 4,
        scratch_shapes=[pltpu.SemaphoreType.DMA((4,))],
        compiler_params=pltpu.CompilerParams(vmem_limit_bytes=2 * 1024 * 1024),
    )(*held)
    return (
        from_rows(volume_next, volume.shape),
        from_rows(split_next, tv_split.shape),
        from_rows(tv_dual_next, tv_dual.shape),
        fit_dual_next.reshape(fit_dual.shape),
    )


def solution(mesh):
    return jax.shard_map(
        shards,
        mesh=mesh,
        in_specs=(
            P(None, ("ang", "slab"), None),
            P(None, None, ("ang", "slab"), None),
            P(None, None, ("ang", "slab"), None),
            P("ang", None, None, None, "slab", None),
            P("ang", None, None, None, "slab", None),
            P(),
            P(),
            P(),
            P(),
        ),
        out_specs=(
            P(None, ("ang", "slab"), None),
            P(None, None, ("ang", "slab"), None),
            P(None, None, ("ang", "slab"), None),
            P("ang", None, None, None, "slab", None),
        ),
        check_vma=False,
    )
```
